256 devices in a mesh: mesh: 64 (over x_hi, z, y), tx: 4 (over x_lo, core).
Axes of the slice: x: 4 (x_hi: 2, x_lo: 2; x = x_hi * 2 + x_lo), y: 4, z: 8, core: 2. Of those that a mesh axis runs over, the one named last changes fastest.
Arguments:
- tx_field: float32 [2, 400, 49152], P(None, 'tx', 'mesh'), may hold values from -6 to 6
- rx_field: float32 [2, 2048, 49152], P(None, 'tx', 'mesh'), may hold values from -6 to 6
- misfit_weight: float32 [2, 400, 2048], P(None, None, 'mesh'), may hold values from -0.0068359375 to 0.0068359375
- incidence: int32 [49152, 4], P('mesh'), may hold values from 0 to 32767, as said below
- component: int32 [49152], P('mesh'), may hold values from 0 to 2
Outputs:
- gradient: float32 [3, 32768], P(None, ('mesh', 'tx'))
The draws below stay inside these ranges and needn't reach their ends.
Inputs may be any that keep to these rules, and one draw needn't show every extreme that they name: `incidence`: the edges of tile i (edges i * 768 to (i + 1) * 768 - 1) name only cells of tiles i - 1, i and i + 1, where tile i holds cells i * 512 to (i + 1) * 512 - 1.
All inputs are finite; a program needn't handle non-finite values.
Results may differ from the reference program's by a relative error of at most 0.00014.
Values sent between devices are 32-bit elements; how exact they have to be, the bound alone decides.
No kernel may reach another device: no remote copies, remote signals or barrier semaphores. Data moves between devices by JAX's collectives and lax.ppermute only.
A program may use at most 64 MiB of HBM per device.

```python
import jax
import jax.numpy as jnp
from jax import lax

NTX = 400
NRX = 2048
EDGE_DEV = 768
CELL_TILE = 512
EDGES = 49152
CELLS = 32768


def draw_incidence(key, part):
    key = jax.random.fold_in(key, 11)
    key_offset, key_roll, key_side = jax.random.split(key, 3)
    tiles = EDGES // EDGE_DEV
    tile = (jnp.arange(EDGES, dtype=jnp.int32) // EDGE_DEV)[:, None]
    offset = jax.random.randint(key_offset, (EDGES, 4), 0, CELL_TILE, dtype=jnp.int32)
    roll = jax.random.randint(key_roll, (EDGES, 4), 0, 100, dtype=jnp.int32)
    side = jax.random.randint(key_side, (EDGES, 4), 0, 2, dtype=jnp.int32) * 2 - 1
    near = jnp.where(roll < 10, side, 0)
    block = jnp.clip(tile + near, 0, tiles - 1)
    cells = block * CELL_TILE + offset
    cells = cells.at[0, 0].set(0)
    cells = cells.at[EDGES - 1, 3].set(tiles * CELL_TILE - 1)
    return cells.astype(jnp.int32)


def place_ends(entries, key, smallest, top_value):
    longest = entries.shape.index(max(entries.shape))
    spots = []
    for shift in (0, 1):
        where = [jax.random.randint(jax.random.fold_in(key, axis), (), 0, length) for axis, length in enumerate(entries.shape)]
        where[longest] = (where[longest] + shift) % entries.shape[longest]
        spots.append(tuple(where))
    return entries.at[spots[0]].set(smallest).at[spots[1]].set(top_value)


def steps_of(rng, extent, shards, smallest, high):
    def one(position, shards_of):
        heights = jax.random.uniform(jax.random.fold_in(jax.random.fold_in(rng, 6), position), (shards_of,), jnp.float32, smallest / len(shards), high / len(shards))
        return jnp.repeat(jnp.exp(heights), extent[position] // shards_of).reshape((-1,) + (1,) * (len(extent) - position - 1))

    loudness = one(*shards[0])
    for cut in shards[1:]:
        loudness = loudness * one(*cut)
    return loudness


def normal_values(key, dims, spread, reach, pieces=(), kind=jnp.bfloat16):
    drawn = spread * jax.random.normal(key, dims, jnp.float32)
    if pieces:
        drawn = drawn * steps_of(key, dims, pieces, -0.22, 0.18)
    return jnp.clip(drawn, -reach, reach).astype(kind)


def setup_inputs(seed: int = 0) -> dict:
    key_list = jax.random.split(jax.random.key(seed), 6)
    tx_field = normal_values(key_list[0], (2, NTX, EDGES), 1.0, 6.0, ((1, 4), (2, 64)), jnp.float32)
    rx_field = normal_values(key_list[1], (2, NRX, EDGES), 1.0, 6.0, ((1, 4), (2, 64)), jnp.float32)
    misfit_weight = normal_values(key_list[2], (2, NTX, NRX), (NTX * NRX) ** -0.5, 0.0068359375, ((2, 64),), jnp.float32)
    incidence = draw_incidence(jax.random.fold_in(key_list[5], 71), 0)
    component = place_ends(jax.random.randint(key_list[4], (EDGES,), 0, 3), jax.random.fold_in(key_list[4], 1), 0, 2).astype(jnp.int32)
    return {"tx_field": tx_field, "rx_field": rx_field, "misfit_weight": misfit_weight, "incidence": incidence, "component": component}


def reference(tx_field, rx_field, misfit_weight, incidence, component):
    high = lax.Precision.HIGHEST
    w_real = misfit_weight[0]
    w_imag = misfit_weight[1]
    q_real = jnp.dot(w_real, rx_field[0], precision=high) - jnp.dot(w_imag, rx_field[1], precision=high)
    q_imag = jnp.dot(w_real, rx_field[1], precision=high) + jnp.dot(w_imag, rx_field[0], precision=high)
    edge_term = jnp.sum(tx_field[0] * q_real - tx_field[1] * q_imag, axis=0)
    flat_index = component[:, None] * CELLS + incidence
    values = jnp.broadcast_to(0.25 * edge_term[:, None], flat_index.shape)
    summed = jax.ops.segment_sum(values.reshape(-1), flat_index.reshape(-1), num_segments=3 * CELLS)
    return summed.reshape(3, CELLS)
```

```python
import functools

import jax
import jax.numpy as jnp
from jax import lax
from jax.experimental import pallas as pl
from jax.experimental.pallas import tpu as pltpu
from jax.sharding import PartitionSpec as P

CELL_TILE = 512
AXES = ("mesh", "tx")
SIZE_Z, SIZE_Y = 8, 4
ROWS = 104
VMEM_LIMIT = 48 * 1024 * 1024


def coords(device):
    mesh_index, tx_index = divmod(device, 4)
    return mesh_index // 32, (mesh_index // 4) % 8, mesh_index % 4, tx_index // 2, tx_index % 2


def device_at(x_hi, z, y, x_lo, core):
    return ((x_hi % 2) * 32 + (z % 8) * 4 + y % 4) * 4 + (x_lo % 2) * 2 + core % 2


def fetch(block, source_of):
    route = [(device_at(*source_of(*coords(d))), d) for d in range(256)]
    return lax.ppermute(block, AXES, route)


def pack_kernel(w_ref, o_ref):
    for part in range(2):
        pieces = [w_ref[part, 100 * g : 100 * (g + 1), :] for g in range(4)]
        o_ref[part, 0:100, :] = jnp.concatenate(pieces, axis=1)
        o_ref[part, 100:ROWS, :] = jnp.zeros((ROWS - 100, 128), jnp.float32)


def pack_weight(misfit_weight):
    return pl.pallas_call(
        pack_kernel,
        out_shape=jax.ShapeDtypeStruct((2, ROWS, 128), jnp.float32),
        name="pack_weight",
    )(misfit_weight)


def split(value):
    high = value.astype(jnp.bfloat16)
    low = (value - high.astype(jnp.float32)).astype(jnp.bfloat16)
    return high, low


def prepare_kernel(place_ref, rx_ref, o_ref):
    real, imag = rx_ref[0], rx_ref[1]
    for n, value in enumerate((real, imag - real, real + imag)):
        high, low = split(value)
        o_ref[0, n, 0] = low
        o_ref[0, n, 1] = high


def prepare_fields(places, rx_field):
    edges = rx_field.shape[2]
    return pl.pallas_call(
        prepare_kernel,
        grid_spec=pltpu.PrefetchScalarGridSpec(
            num_scalar_prefetch=1,
            grid=(16,),
            in_specs=[pl.BlockSpec((2, 32, edges), lambda i, place: (0, place[i], 0))],
            out_specs=pl.BlockSpec((1, 3, 2, 32, edges), lambda i, place: (i // 8, 0, 0, i % 8, 0)),
        ),
        out_shape=jax.ShapeDtypeStruct((2, 3, 2, 256, edges), jnp.bfloat16),
        cost_estimate=pl.CostEstimate(flops=10_000_000, bytes_accessed=8_000_000, transcendentals=0),
        name="prepare_fields",
    )(places, rx_field)


def lane_group():
    return lax.broadcasted_iota(jnp.int32, (ROWS, 128), 1) // 32


def product_kernel(
    index_ref, own0, own1, above, below, far0, far1, t0, t1, t2, t3, field, before, o_ref, w_scr, wh_scr, wl_scr
):
    tx_index = index_ref[0]
    group = lane_group()
    own, far, txs = (own0, own1), (far0, far1), (t0, t1, t2, t3)
    for part in range(2):
        for k in range(2):
            blocks = [own[k][part], above[k, part], far[k][part], below[k, part]]
            rolled = [b if s == 0 else pltpu.roll(b, 32 * s, 1) for s, b in enumerate(blocks)]
            for g in range(4):
                mixed = rolled[(0 - g) % 4]
                for lane in range(1, 4):
                    mixed = jnp.where(group == lane, rolled[(lane - g) % 4], mixed)
                if g:
                    mixed = pltpu.roll(mixed, 128 - 32 * g, 1)
                row = pl.multiple_of(jnp.bitwise_xor(tx_index, g) * ROWS, 8)
                w_scr[part, pl.ds(row, ROWS), 128 * k : 128 * (k + 1)] = mixed
    real, imag = w_scr[0], w_scr[1]
    for n, value in enumerate((real + imag, real, imag)):
        high, low = split(value)
        wh_scr[n, :, 0:256] = high
        wh_scr[n, :, 256:512] = high
        wl_scr[n] = low
    for tile in range(field.shape[4] // 256):
        cols = slice(256 * tile, 256 * (tile + 1))
        products = []
        for n in range(3):
            both = field[0, n, :, :, cols].reshape(512, 256)
            high = field[0, n, 1, :, cols]
            products.append(
                jnp.dot(wh_scr[n], both, preferred_element_type=jnp.float32)
                + jnp.dot(wl_scr[n], high, preferred_element_type=jnp.float32)
            )
        total = before[:, cols]
        for g in range(4):
            rows = slice(ROWS * g, ROWS * g + 100)
            a, b = txs[g][0, :, cols], txs[g][1, :, cols]
            term = (a - b) * products[0][rows] - b * products[1][rows] - a * products[2][rows]
            total = total + jnp.sum(term, axis=0, keepdims=True)
        o_ref[:, cols] = total


def product(index, blocks, txs, fields, group, before):
    edges = fields.shape[4]
    whole = pl.BlockSpec(memory_space=pltpu.VMEM)
    return pl.pallas_call(
        product_kernel,
        grid_spec=pltpu.PrefetchScalarGridSpec(
            num_scalar_prefetch=1,
            grid=(1,),
            in_specs=[whole] * 10 + [pl.BlockSpec((1, 3, 2, 256, edges), lambda i, s: (group, 0, 0, 0, 0)), whole],
            out_specs=whole,
            scratch_shapes=[
                pltpu.VMEM((2, 4 * ROWS, 256), jnp.float32),
                pltpu.VMEM((3, 4 * ROWS, 512), jnp.bfloat16),
                pltpu.VMEM((3, 4 * ROWS, 256), jnp.bfloat16),
            ],
        ),
        out_shape=jax.ShapeDtypeStruct((1, edges), jnp.float32),
        compiler_params=pltpu.CompilerParams(vmem_limit_bytes=VMEM_LIMIT),
        cost_estimate=pl.CostEstimate(flops=3_000_000_000, bytes_accessed=6_000_000, transcendentals=0),
        name="product",
    )(index, *blocks, *txs, fields, before)


def onehot_kernel(index_ref, cells_ref, cells_t_ref, component_ref, hot_ref, row_ref):
    base, tx_index = index_ref[1], index_ref[0]
    lanes = lax.broadcasted_iota(jnp.int32, (cells_ref.shape[0], 128), 1)
    for j in range(4):
        lane = jnp.bitwise_and(cells_ref[:, j : j + 1], 127)
        hot_ref[j] = jnp.where(lanes == lane, 1.0, 0.0).astype(jnp.bfloat16)
    block = (cells_t_ref[...] - base) >> 7
    row = component_ref[...] * 3 + (block >> 2)
    row_ref[...] = jnp.where(jnp.bitwise_and(block, 3) == tx_index, row, -1)


def onehots(index, incidence, component):
    edges = incidence.shape[0]
    whole = pl.BlockSpec(memory_space=pltpu.VMEM)
    return pl.pallas_call(
        onehot_kernel,
        in_specs=[pl.BlockSpec(memory_space=pltpu.SMEM), whole, whole, whole],
        out_shape=(
            jax.ShapeDtypeStruct((4, edges, 128), jnp.bfloat16),
            jax.ShapeDtypeStruct((4, edges), jnp.int32),
        ),
        name="onehots",
    )(index, incidence, incidence.T, component[None, :])


def scatter_kernel(e0, e1, e2, e3, hot_ref, row_ref, low_ref, mid_ref, high_ref):
    total = 0.25 * ((e0[...] + e1[...]) + (e2[...] + e3[...]))
    edges = total.shape[1]
    rows = lax.broadcasted_iota(jnp.int32, (16, edges), 0)
    first = total.astype(jnp.bfloat16).astype(jnp.float32)
    rest = total - first
    second = rest.astype(jnp.bfloat16).astype(jnp.float32)
    third = rest - second
    summed = jnp.zeros((48, 128), jnp.float32)
    for j in range(4):
        hit = rows == row_ref[j : j + 1, :]
        left = jnp.concatenate([jnp.where(hit, v, 0.0) for v in (first, second, third)], axis=0)
        summed += jnp.dot(left.astype(jnp.bfloat16), hot_ref[j], preferred_element_type=jnp.float32)
    cells = (summed[0:16] + summed[16:32]) + summed[32:48]
    for k in range(3):
        low_ref[k : k + 1, :] = cells[3 * k : 3 * k + 1, :]
        mid_ref[k : k + 1, :] = cells[3 * k + 1 : 3 * k + 2, :]
        high_ref[k : k + 1, :] = cells[3 * k + 2 : 3 * k + 3, :]


def scatter(terms, hot, row):
    return pl.pallas_call(
        scatter_kernel,
        out_shape=[jax.ShapeDtypeStruct((3, 128), jnp.float32)] * 3,
        name="scatter_cells",
    )(*terms, hot, row)


def passed_along(block, distance):
    route = [((i - distance) * 4 + j, i * 4 + j) for i in range(64) for j in range(4) if 0 <= i - distance < 64]
    return lax.ppermute(block, AXES, route)


def flip_x(x_hi, z, y, x_lo, core):
    return x_hi, z, y, 1 - x_lo, core


def flip_core(x_hi, z, y, x_lo, core):
    return x_hi, z, y, x_lo, 1 - core


def flip_both(x_hi, z, y, x_lo, core):
    return x_hi, z, y, 1 - x_lo, 1 - core


def z_source(k):
    return lambda x_hi, z, y, x_lo, core: (x_lo, 4 * core + (z + k) % 4, y, x_hi, z // 4)


def y_source(step):
    return lambda x_hi, z, y, x_lo, core: (x_hi, z, y + step, x_lo, core)


def shards(tx_field, rx_field, misfit_weight, incidence, component):
    mesh_index = lax.axis_index("mesh")
    tx_index = lax.axis_index("tx")
    z, y = (mesh_index // 4) % 8, mesh_index % 4
    packed = pack_weight(misfit_weight)
    tx_x = fetch(tx_field, flip_x)
    from_z = [fetch(packed, z_source(k)) for k in range(4)]
    tx_c = fetch(tx_field, flip_core)
    tx_xc = fetch(tx_x, flip_core)
    txs = [tx_field, tx_c, tx_x, tx_xc]

    steps = jnp.arange(16, dtype=jnp.int32)
    places = ((z + steps // 4) % 4) * 4 + (y + steps % 4) % 4
    fields = prepare_fields(places.astype(jnp.int32), rx_field)
    index = jnp.stack([tx_index, (mesh_index - 1) * CELL_TILE]).astype(jnp.int32)
    hot, row = onehots(index, incidence, component)

    edge = jnp.zeros((1, tx_field.shape[2]), jnp.float32)
    for group in range(2):
        own = from_z[2 * group : 2 * group + 2]
        stacked = jnp.stack(own)
        above = fetch(stacked, y_source(1))
        below = fetch(stacked, y_source(-1))
        far0 = fetch(above[0], y_source(1))
        far1 = fetch(below[1], y_source(-1))
        blocks = [own[0], own[1], above, below, far0, far1]
        edge = product(index, blocks, txs, fields, group, edge)
    terms = [edge, fetch(edge, flip_core), fetch(edge, flip_x), fetch(edge, flip_both)]
    low, mid, high = scatter(terms, hot, row)
    return mid + passed_along(low, -1) + passed_along(high, 1)


def solution(mesh):
    return jax.shard_map(
        shards,
        mesh=mesh,
        in_specs=(
            P(None, "tx", "mesh"),
            P(None, "tx", "mesh"),
            P(None, None, "mesh"),
            P("mesh", None),
            P("mesh"),
        ),
        out_specs=P(None, ("mesh", "tx")),
        check_vma=False,
    )
```

```python
import functools

import jax
import jax.numpy as jnp
from jax import lax
from jax.experimental import pallas as pl
from jax.experimental.pallas import tpu as pltpu
from jax.sharding import PartitionSpec as P

CELL_TILE = 512
AXES = ("mesh", "tx")
SIZE_Z, SIZE_Y = 8, 4
ROWS = 104
VMEM_LIMIT = 48 * 1024 * 1024


def coords(device):
    mesh_index, tx_index = divmod(device, 4)
    return mesh_index // 32, (mesh_index // 4) % 8, mesh_index % 4, tx_index // 2, tx_index % 2


def device_at(x_hi, z, y, x_lo, core):
    return ((x_hi % 2) * 32 + (z % 8) * 4 + y % 4) * 4 + (x_lo % 2) * 2 + core % 2


def fetch(block, source_of):
    route = [(device_at(*source_of(*coords(d))), d) for d in range(256)]
    return lax.ppermute(block, AXES, route)


def pack_kernel(w_ref, o_ref):
    for part in range(2):
        value = w_ref[part].T
        pieces = [value[100 * g : 100 * (g + 1), :] for g in range(4)]
        o_ref[part, 0:100, :] = jnp.concatenate(pieces, axis=1)
        o_ref[part, 100:ROWS, :] = jnp.zeros((ROWS - 100, 128), jnp.float32)


def pack_weight(misfit_weight):
    return pl.pallas_call(
        pack_kernel,
        out_shape=jax.ShapeDtypeStruct((2, ROWS, 128), jnp.float32),
        name="pack_weight",
    )(misfit_weight.transpose(0, 2, 1))


def split(value):
    high = value.astype(jnp.bfloat16)
    low = (value - high.astype(jnp.float32)).astype(jnp.bfloat16)
    return high, low


def prepare_kernel(place_ref, rx_ref, o_ref):
    for s in range(4):
        row = pl.multiple_of(place_ref[4 + s] * 32, 32)
        real, imag = rx_ref[0, pl.ds(row, 32), :], rx_ref[1, pl.ds(row, 32), :]
        for n, value in enumerate((real, imag - real, real + imag)):
            high, low = split(value)
            o_ref[0, n, 0, 32 * s : 32 * (s + 1), :] = low
            o_ref[0, n, 1, 32 * s : 32 * (s + 1), :] = high


def prepare_fields(places, rx_field):
    edges = rx_field.shape[2]
    return pl.pallas_call(
        prepare_kernel,
        grid_spec=pltpu.PrefetchScalarGridSpec(
            num_scalar_prefetch=1,
            grid=(4,),
            in_specs=[pl.BlockSpec((2, 128, edges), lambda i, place: (0, place[i], 0))],
            out_specs=pl.BlockSpec((1, 3, 2, 128, edges), lambda i, place: (i // 2, 0, 0, i % 2, 0)),
        ),
        out_shape=jax.ShapeDtypeStruct((2, 3, 2, 256, edges), jnp.bfloat16),
        compiler_params=pltpu.CompilerParams(vmem_limit_bytes=VMEM_LIMIT),
        cost_estimate=pl.CostEstimate(flops=10_000_000, bytes_accessed=8_000_000, transcendentals=0),
        name="prepare_fields",
    )(places, rx_field)


def lane_group():
    return lax.broadcasted_iota(jnp.int32, (ROWS, 128), 1) // 32


def product_kernel(
    index_ref, own0, own1, above, below, far0, far1, t0, t1, t2, t3, field, before, o_ref, w_scr, wh_scr, wl_scr
):
    tx_index = index_ref[0]
    group = lane_group()
    own, far, txs = (own0, own1), (far0, far1), (t0, t1, t2, t3)
    for part in range(2):
        for k in range(2):
            blocks = [own[k][part], above[k, part], far[k][part], below[k, part]]
            rolled = [b if s == 0 else pltpu.roll(b, 32 * s, 1) for s, b in enumerate(blocks)]
            for g in range(4):
                mixed = rolled[(0 - g) % 4]
                for lane in range(1, 4):
                    mixed = jnp.where(group == lane, rolled[(lane - g) % 4], mixed)
                if g:
                    mixed = pltpu.roll(mixed, 128 - 32 * g, 1)
                row = pl.multiple_of(jnp.bitwise_xor(tx_index, g) * ROWS, 8)
                w_scr[part, pl.ds(row, ROWS), 128 * k : 128 * (k + 1)] = mixed
    real, imag = w_scr[0], w_scr[1]
    for n, value in enumerate((real + imag, real, imag)):
        high, low = split(value)
        wh_scr[n, :, 0:256] = high
        wh_scr[n, :, 256:512] = high
        wl_scr[n] = low
    for tile in range(field.shape[4] // 256):
        cols = slice(256 * tile, 256 * (tile + 1))
        products = []
        for n in range(3):
            both = field[0, n, :, :, cols].reshape(512, 256)
            high = field[0, n, 1, :, cols]
            products.append(
                jnp.dot(wh_scr[n], both, preferred_element_type=jnp.float32)
                + jnp.dot(wl_scr[n], high, preferred_element_type=jnp.float32)
            )
        total = before[:, cols]
        for g in range(4):
            rows = slice(ROWS * g, ROWS * g + 100)
            a, b = txs[g][0, :, cols], txs[g][1, :, cols]
            term = (a - b) * products[0][rows] - b * products[1][rows] - a * products[2][rows]
            total = total + jnp.sum(term, axis=0, keepdims=True)
        o_ref[:, cols] = total


def product(index, blocks, txs, fields, group, before):
    edges = fields.shape[4]
    whole = pl.BlockSpec(memory_space=pltpu.VMEM)
    return pl.pallas_call(
        product_kernel,
        grid_spec=pltpu.PrefetchScalarGridSpec(
            num_scalar_prefetch=1,
            grid=(1,),
            in_specs=[whole] * 10 + [pl.BlockSpec((1, 3, 2, 256, edges), lambda i, s: (group, 0, 0, 0, 0)), whole],
            out_specs=whole,
            scratch_shapes=[
                pltpu.VMEM((2, 4 * ROWS, 256), jnp.float32),
                pltpu.VMEM((3, 4 * ROWS, 512), jnp.bfloat16),
                pltpu.VMEM((3, 4 * ROWS, 256), jnp.bfloat16),
            ],
        ),
        out_shape=jax.ShapeDtypeStruct((1, edges), jnp.float32),
        compiler_params=pltpu.CompilerParams(vmem_limit_bytes=VMEM_LIMIT),
        cost_estimate=pl.CostEstimate(flops=3_000_000_000, bytes_accessed=6_000_000, transcendentals=0),
        name="product",
    )(index, *blocks, *txs, fields, before)


def onehot_kernel(index_ref, cells_ref, component_ref, hot_ref, row_ref):
    x_lo, core, base = index_ref[1], index_ref[2], index_ref[3]
    cells = cells_ref[...] - base
    edges = cells.shape[1]
    lanes = lax.broadcasted_iota(jnp.int32, (128, edges), 0)
    for j in range(4):
        hit = lanes == jnp.bitwise_and(cells[j : j + 1, :], 127)
        hot_ref[j] = jnp.where(hit, 1.0, 0.0).astype(jnp.bfloat16)
    block = cells >> 7
    row = component_ref[...] * 3
    other = 8 * core + 2 * x_lo
    row_ref[...] = jnp.where(
        block == 4 + 2 * x_lo + core,
        row,
        jnp.where(block == other + core, row + 1, jnp.where(block == other + 1 - core, row + 2, -1)),
    )


def onehots(index, incidence, component):
    edges = incidence.shape[0]
    whole = pl.BlockSpec(memory_space=pltpu.VMEM)
    return pl.pallas_call(
        onehot_kernel,
        in_specs=[pl.BlockSpec(memory_space=pltpu.SMEM), whole, whole],
        out_shape=(
            jax.ShapeDtypeStruct((4, 128, edges), jnp.bfloat16),
            jax.ShapeDtypeStruct((4, edges), jnp.int32),
        ),
        name="onehots",
    )(index, incidence.T, component[None, :])


def scatter_kernel(e0, e1, e2, e3, hot_ref, row_ref, own_ref, send_ref):
    total = 0.25 * ((e0[...] + e1[...]) + (e2[...] + e3[...]))
    edges = total.shape[1]
    rows = lax.broadcasted_iota(jnp.int32, (16, edges), 0)
    first = total.astype(jnp.bfloat16).astype(jnp.float32)
    rest = total - first
    second = rest.astype(jnp.bfloat16).astype(jnp.float32)
    third = rest - second
    summed = jnp.zeros((48, 128), jnp.float32)
    for j in range(4):
        hit = rows == row_ref[j : j + 1, :]
        left = jnp.concatenate([jnp.where(hit, v, 0.0) for v in (first, second, third)], axis=0)
        summed += lax.dot_general(
            left.astype(jnp.bfloat16), hot_ref[j], (((1,), (1,)), ((), ())), preferred_element_type=jnp.float32
        )
    cells = (summed[0:16] + summed[16:32]) + summed[32:48]
    for k in range(3):
        own_ref[k : k + 1, :] = cells[3 * k : 3 * k + 1, :]
        send_ref[0, k : k + 1, :] = cells[3 * k + 1 : 3 * k + 2, :]
        send_ref[1, k : k + 1, :] = cells[3 * k + 2 : 3 * k + 3, :]


def scatter(terms, hot, row):
    return pl.pallas_call(
        scatter_kernel,
        out_shape=(jax.ShapeDtypeStruct((3, 128), jnp.float32), jax.ShapeDtypeStruct((2, 3, 128), jnp.float32)),
        name="scatter_cells",
    )(*terms, hot, row)


def neighbour_parts(block):
    route = []
    for m in range(64):
        for j in range(4):
            source = m + 1 if j % 2 == 0 else m - 1
            if 0 <= source < 64:
                route.append((source * 4 + j, m * 4 + j))
    return lax.ppermute(block, AXES, route)


def flip_x(x_hi, z, y, x_lo, core):
    return x_hi, z, y, 1 - x_lo, core


def flip_core(x_hi, z, y, x_lo, core):
    return x_hi, z, y, x_lo, 1 - core


def flip_both(x_hi, z, y, x_lo, core):
    return x_hi, z, y, 1 - x_lo, 1 - core


def z_source(k):
    return lambda x_hi, z, y, x_lo, core: (x_lo, 4 * core + (z + k) % 4, y, x_hi, z // 4)


def y_source(step):
    return lambda x_hi, z, y, x_lo, core: (x_hi, z, y + step, x_lo, core)


def shards(tx_field, rx_field, misfit_weight, incidence, component):
    mesh_index = lax.axis_index("mesh")
    tx_index = lax.axis_index("tx")
    z, y = (mesh_index // 4) % 8, mesh_index % 4
    packed = pack_weight(misfit_weight)
    tx_x = fetch(tx_field, flip_x)
    from_z = [fetch(packed, z_source(k)) for k in range(4)]
    tx_c = fetch(tx_field, flip_core)
    tx_xc = fetch(tx_x, flip_core)
    txs = [tx_field, tx_c, tx_x, tx_xc]

    steps = jnp.arange(4, dtype=jnp.int32)
    places = jnp.concatenate([(z + steps) % 4, (y + steps) % 4]).astype(jnp.int32)
    fields = prepare_fields(places, rx_field)
    index = jnp.stack([tx_index, tx_index // 2, tx_index % 2, (mesh_index - 1) * CELL_TILE]).astype(jnp.int32)
    hot, row = onehots(index, incidence, component)

    edge = jnp.zeros((1, tx_field.shape[2]), jnp.float32)
    for group in range(2):
        own = from_z[2 * group : 2 * group + 2]
        stacked = jnp.stack(own)
        above = fetch(stacked, y_source(1))
        below = fetch(stacked, y_source(-1))
        far0 = fetch(above[0], y_source(1))
        far1 = fetch(below[1], y_source(-1))
        blocks = [own[0], own[1], above, below, far0, far1]
        edge = product(index, blocks, txs, fields, group, edge)
    terms = [edge, fetch(edge, flip_core), fetch(edge, flip_x), fetch(edge, flip_both)]
    own, send = scatter(terms, hot, row)
    received = neighbour_parts(send)
    return own + received[0] + fetch(received[1], flip_core)


def solution(mesh):
    return jax.shard_map(
        shards,
        mesh=mesh,
        in_specs=(
            P(None, "tx", "mesh"),
            P(None, "tx", "mesh"),
            P(None, None, "mesh"),
            P("mesh", None),
            P("mesh"),
        ),
        out_specs=P(None, ("mesh", "tx")),
        check_vma=False,
    )
```

```python
import functools

import jax
import jax.numpy as jnp
from jax import lax
from jax.experimental import pallas as pl
from jax.experimental.pallas import tpu as pltpu
from jax.sharding import PartitionSpec as P

CELL_TILE = 512
AXES = ("mesh", "tx")
SIZE_Z, SIZE_Y = 8, 4
ROWS = 104
MIB = 1024 * 1024
WHOLE = pl.BlockSpec(memory_space=pltpu.VMEM)
SCALARS = pl.BlockSpec(memory_space=pltpu.SMEM)


def limit(mib):
    return pltpu.CompilerParams(vmem_limit_bytes=mib * MIB)


def coords(device):
    mesh_index, tx_index = divmod(device, 4)
    return mesh_index // 32, (mesh_index // 4) % 8, mesh_index % 4, tx_index // 2, tx_index % 2


def device_at(x_hi, z, y, x_lo, core):
    return ((x_hi % 2) * 32 + (z % 8) * 4 + y % 4) * 4 + (x_lo % 2) * 2 + core % 2


def fetch(block, source_of):
    route = [(device_at(*source_of(*coords(d))), d) for d in range(256)]
    return lax.ppermute(block, AXES, route)


def pack_kernel(w_ref, o_ref):
    for part in range(2):
        value = w_ref[part].T
        pieces = [value[100 * g : 100 * (g + 1), :] for g in range(4)]
        o_ref[part, 0:100, :] = jnp.concatenate(pieces, axis=1)
        o_ref[part, 100:ROWS, :] = jnp.zeros((ROWS - 100, 128), jnp.float32)


def pack_weight(misfit_weight):
    return pl.pallas_call(
        pack_kernel,
        in_specs=[WHOLE],
        out_specs=WHOLE,
        out_shape=jax.ShapeDtypeStruct((2, ROWS, 128), jnp.float32),
        compiler_params=limit(2),
        name="pack_weight",
    )(misfit_weight.transpose(0, 2, 1))


def split(value):
    high = value.astype(jnp.bfloat16)
    low = (value - high.astype(jnp.float32)).astype(jnp.bfloat16)
    return high, low


def prepare_kernel(place_ref, rx_ref, o_ref):
    for k in range(4):
        for s in range(4):
            row = pl.multiple_of(place_ref[k] * 128 + place_ref[4 + s] * 32, 32)
            real, imag = rx_ref[0, pl.ds(row, 32), :], rx_ref[1, pl.ds(row, 32), :]
            rows = slice(128 * (k % 2) + 32 * s, 128 * (k % 2) + 32 * (s + 1))
            for n, value in enumerate((real, imag - real, real + imag)):
                high, low = split(value)
                o_ref[k // 2, n, 0, rows, :] = low
                o_ref[k // 2, n, 1, rows, :] = high


def prepare_fields(places, rx_field):
    edges = rx_field.shape[2]
    return pl.pallas_call(
        prepare_kernel,
        in_specs=[SCALARS, WHOLE],
        out_specs=WHOLE,
        out_shape=jax.ShapeDtypeStruct((2, 3, 2, 256, edges), jnp.bfloat16),
        compiler_params=limit(4),
        cost_estimate=pl.CostEstimate(flops=10_000_000, bytes_accessed=8_000_000, transcendentals=0),
        name="prepare_fields",
    )(places, rx_field)


def arrange_kernel(after_ref, tx_ref, o_ref):
    o_ref[0] = tx_ref[:, 0, :]
    o_ref[1] = tx_ref[:, 1, :]


def arrange(after, tx_field):
    return pl.pallas_call(
        arrange_kernel,
        in_specs=[pl.BlockSpec(memory_space=pl.ANY), WHOLE],
        out_specs=WHOLE,
        out_shape=jax.ShapeDtypeStruct(tx_field.shape, jnp.float32),
        compiler_params=limit(4),
        name="arrange",
    )(after, tx_field.transpose(1, 0, 2))


def lane_group():
    return lax.broadcasted_iota(jnp.int32, (ROWS, 128), 1) // 32


def product_kernel(
    group_index, index_ref, own0, own1, above, below, far0, far1, t0, t1, t2, t3, field, before, o_ref, w_scr, wh_scr, wl_scr
):
    tx_index = index_ref[0]
    group = lane_group()
    own, far, txs = (own0, own1), (far0, far1), (t0, t1, t2, t3)
    for part in range(2):
        for k in range(2):
            blocks = [own[k][part], above[k, part], far[k][part], below[k, part]]
            rolled = [b if s == 0 else pltpu.roll(b, 32 * s, 1) for s, b in enumerate(blocks)]
            for g in range(4):
                mixed = rolled[(0 - g) % 4]
                for lane in range(1, 4):
                    mixed = jnp.where(group == lane, rolled[(lane - g) % 4], mixed)
                if g:
                    mixed = pltpu.roll(mixed, 128 - 32 * g, 1)
                row = pl.multiple_of(jnp.bitwise_xor(tx_index, g) * ROWS, 8)
                w_scr[part, pl.ds(row, ROWS), 128 * k : 128 * (k + 1)] = mixed
    real, imag = w_scr[0], w_scr[1]
    for n, value in enumerate((real + imag, real, imag)):
        high, low = split(value)
        wh_scr[n, :, 0:256] = high
        wh_scr[n, :, 256:512] = high
        wl_scr[n] = low
    for tile in range(field.shape[4] // 256):
        cols = slice(256 * tile, 256 * (tile + 1))
        products = []
        for n in range(3):
            both = field[group_index, n, :, :, cols].reshape(512, 256)
            high = field[group_index, n, 1, :, cols]
            products.append(
                jnp.dot(wh_scr[n], both, preferred_element_type=jnp.float32)
                + jnp.dot(wl_scr[n], high, preferred_element_type=jnp.float32)
            )
        total = before[:, cols]
        for g in range(4):
            rows = slice(ROWS * g, ROWS * g + 100)
            a, b = txs[g][0, :, cols], txs[g][1, :, cols]
            term = (a - b) * products[0][rows] - b * products[1][rows] - a * products[2][rows]
            total = total + jnp.sum(term, axis=0, keepdims=True)
        o_ref[:, cols] = total


def product(index, blocks, txs, fields, group, before):
    edges = fields.shape[4]
    return pl.pallas_call(
        functools.partial(product_kernel, group),
        in_specs=[SCALARS] + [WHOLE] * 12,
        out_specs=WHOLE,
        scratch_shapes=[
            pltpu.VMEM((2, 4 * ROWS, 256), jnp.float32),
            pltpu.VMEM((3, 4 * ROWS, 512), jnp.bfloat16),
            pltpu.VMEM((3, 4 * ROWS, 256), jnp.bfloat16),
        ],
        out_shape=jax.ShapeDtypeStruct((1, edges), jnp.float32),
        compiler_params=limit(12),
        cost_estimate=pl.CostEstimate(flops=3_000_000_000, bytes_accessed=6_000_000, transcendentals=0),
        name="product",
    )(index, *blocks, *txs, fields, before)


def onehot_kernel(index_ref, cells_ref, component_ref, hot_ref, row_ref):
    x_lo, core, base = index_ref[1], index_ref[2], index_ref[3]
    cells = cells_ref[...] - base
    edges = cells.shape[1]
    lanes = lax.broadcasted_iota(jnp.int32, (128, edges), 0)
    for j in range(4):
        hit = lanes == jnp.bitwise_and(cells[j : j + 1, :], 127)
        hot_ref[j] = jnp.where(hit, 1.0, 0.0).astype(jnp.bfloat16)
    block = cells >> 7
    row = component_ref[...] * 3
    other = 8 * core + 2 * x_lo
    row_ref[...] = jnp.where(
        block == 4 + 2 * x_lo + core,
        row,
        jnp.where(block == other + core, row + 1, jnp.where(block == other + 1 - core, row + 2, -1)),
    )


def onehots(index, incidence, component):
    edges = incidence.shape[0]
    return pl.pallas_call(
        onehot_kernel,
        in_specs=[SCALARS, WHOLE, WHOLE],
        out_specs=(WHOLE, WHOLE),
        compiler_params=limit(2),
        out_shape=(
            jax.ShapeDtypeStruct((4, 128, edges), jnp.bfloat16),
            jax.ShapeDtypeStruct((4, edges), jnp.int32),
        ),
        name="onehots",
    )(index, incidence.T, component[None, :])


def scatter_kernel(e0, e1, e2, e3, hot_ref, row_ref, own_ref, send_ref):
    total = 0.25 * ((e0[...] + e1[...]) + (e2[...] + e3[...]))
    edges = total.shape[1]
    rows = lax.broadcasted_iota(jnp.int32, (16, edges), 0)
    first = total.astype(jnp.bfloat16).astype(jnp.float32)
    rest = total - first
    second = rest.astype(jnp.bfloat16).astype(jnp.float32)
    third = rest - second
    summed = jnp.zeros((48, 128), jnp.float32)
    for j in range(4):
        hit = rows == row_ref[j : j + 1, :]
        left = jnp.concatenate([jnp.where(hit, v, 0.0) for v in (first, second, third)], axis=0)
        summed += lax.dot_general(
            left.astype(jnp.bfloat16), hot_ref[j], (((1,), (1,)), ((), ())), preferred_element_type=jnp.float32
        )
    cells = (summed[0:16] + summed[16:32]) + summed[32:48]
    for k in range(3):
        own_ref[k : k + 1, :] = cells[3 * k : 3 * k + 1, :]
        send_ref[0, k : k + 1, :] = cells[3 * k + 1 : 3 * k + 2, :]
        send_ref[1, k : k + 1, :] = cells[3 * k + 2 : 3 * k + 3, :]


def scatter(terms, hot, row):
    return pl.pallas_call(
        scatter_kernel,
        in_specs=[WHOLE] * 6,
        out_specs=(WHOLE, WHOLE),
        compiler_params=limit(4),
        out_shape=(jax.ShapeDtypeStruct((3, 128), jnp.float32), jax.ShapeDtypeStruct((2, 3, 128), jnp.float32)),
        name="scatter_cells",
    )(*terms, hot, row)


def total_kernel(own_ref, received_ref, passed_ref, o_ref):
    o_ref[...] = own_ref[...] + received_ref[0] + passed_ref[...]


def total(own, received, passed):
    return pl.pallas_call(
        total_kernel,
        in_specs=[WHOLE] * 3,
        out_specs=WHOLE,
        compiler_params=limit(2),
        out_shape=jax.ShapeDtypeStruct(own.shape, jnp.float32),
        name="total",
    )(own, received, passed)


def neighbour_parts(block):
    route = []
    for m in range(64):
        for j in range(4):
            source = m + 1 if j % 2 == 0 else m - 1
            if 0 <= source < 64:
                route.append((source * 4 + j, m * 4 + j))
    return lax.ppermute(block, AXES, route)


def flip_x(x_hi, z, y, x_lo, core):
    return x_hi, z, y, 1 - x_lo, core


def flip_core(x_hi, z, y, x_lo, core):
    return x_hi, z, y, x_lo, 1 - core


def flip_both(x_hi, z, y, x_lo, core):
    return x_hi, z, y, 1 - x_lo, 1 - core


def z_source(k):
    return lambda x_hi, z, y, x_lo, core: (x_lo, 4 * core + (z + k) % 4, y, x_hi, z // 4)


def y_source(step):
    return lambda x_hi, z, y, x_lo, core: (x_hi, z, y + step, x_lo, core)


def shards(tx_field, rx_field, misfit_weight, incidence, component):
    mesh_index = lax.axis_index("mesh")
    tx_index = lax.axis_index("tx")
    z, y = (mesh_index // 4) % 8, mesh_index % 4
    packed = pack_weight(misfit_weight)
    tx_x = fetch(tx_field, flip_x)
    from_z = [fetch(packed, z_source(k)) for k in range(4)]
    steps = jnp.arange(4, dtype=jnp.int32)
    places = jnp.concatenate([(z + steps) % 4, (y + steps) % 4]).astype(jnp.int32)
    fields = prepare_fields(places, rx_field)
    tx_own = arrange(fields, tx_field)
    txs = [tx_own, fetch(tx_own, flip_core), tx_x, fetch(tx_x, flip_core)]
    index = jnp.stack([tx_index, tx_index // 2, tx_index % 2, (mesh_index - 1) * CELL_TILE]).astype(jnp.int32)
    hot, row = onehots(index, incidence, component)

    edge = jnp.zeros((1, tx_field.shape[2]), jnp.float32)
    for group in range(2):
        own = from_z[2 * group : 2 * group + 2]
        stacked = jnp.stack(own)
        above = fetch(stacked, y_source(1))
        below = fetch(stacked, y_source(-1))
        far0 = fetch(above[0], y_source(1))
        far1 = fetch(below[1], y_source(-1))
        blocks = [own[0], own[1], above, below, far0, far1]
        edge = product(index, blocks, txs, fields, group, edge)
    terms = [edge, fetch(edge, flip_core), fetch(edge, flip_x), fetch(edge, flip_both)]
    own, send = scatter(terms, hot, row)
    received = neighbour_parts(send)
    return total(own, received, fetch(received[1], flip_core))


def solution(mesh):
    return jax.shard_map(
        shards,
        mesh=mesh,
        in_specs=(
            P(None, "tx", "mesh"),
            P(None, "tx", "mesh"),
            P(None, None, "mesh"),
            P("mesh", None),
            P("mesh"),
        ),
        out_specs=P(None, ("mesh", "tx")),
        check_vma=False,
    )
```

```python
import functools

import jax
import jax.numpy as jnp
from jax import lax
from jax.experimental import pallas as pl
from jax.experimental.pallas import tpu as pltpu
from jax.sharding import PartitionSpec as P

CELL_TILE = 512
AXES = ("mesh", "tx")
SIZE_Z, SIZE_Y = 8, 4
TURNS = (0, 1, 2, 3)
ROWS = 104
MIB = 1024 * 1024
WHOLE = pl.BlockSpec(memory_space=pltpu.VMEM)
SCALARS = pl.BlockSpec(memory_space=pltpu.SMEM)


def limit(mib):
    return pltpu.CompilerParams(vmem_limit_bytes=mib * MIB)


def coords(device):
    mesh_index, tx_index = divmod(device, 4)
    return mesh_index // 32, (mesh_index // 4) % 8, mesh_index % 4, tx_index // 2, tx_index % 2


def device_at(x_hi, z, y, x_lo, core):
    return ((x_hi % 2) * 32 + (z % 8) * 4 + y % 4) * 4 + (x_lo % 2) * 2 + core % 2


def fetch(block, source_of):
    route = [(device_at(*source_of(*coords(d))), d) for d in range(256)]
    return lax.ppermute(block, AXES, route)


def pack_kernel(w_ref, o_ref):
    for part in range(2):
        value = w_ref[part].T
        pieces = [value[100 * g : 100 * (g + 1), :] for g in range(4)]
        o_ref[part, 0:100, :] = jnp.concatenate(pieces, axis=1)
        o_ref[part, 100:ROWS, :] = jnp.zeros((ROWS - 100, 128), jnp.float32)


def pack_weight(misfit_weight):
    return pl.pallas_call(
        pack_kernel,
        in_specs=[WHOLE],
        out_specs=WHOLE,
        out_shape=jax.ShapeDtypeStruct((2, ROWS, 128), jnp.float32),
        compiler_params=limit(2),
        name="pack_weight",
    )(misfit_weight.transpose(0, 2, 1))


def split(value):
    high = value.astype(jnp.bfloat16)
    low = (value - high.astype(jnp.float32)).astype(jnp.bfloat16)
    return high, low


def prepare_kernel(place_ref, after_ref, rx_ref, o_ref):
    for s in range(4):
        for k in range(4):
            row = pl.multiple_of(place_ref[k] * 128 + place_ref[4 + s] * 32, 32)
            real, imag = rx_ref[0, pl.ds(row, 32), :], rx_ref[1, pl.ds(row, 32), :]
            rows = slice(128 * (s % 2) + 32 * k, 128 * (s % 2) + 32 * (k + 1))
            for n, value in enumerate((real, imag - real, real + imag)):
                high, low = split(value)
                o_ref[s // 2, n, 0, rows, :] = low
                o_ref[s // 2, n, 1, rows, :] = high


def prepare_fields(places, after, rx_field):
    edges = rx_field.shape[2]
    return pl.pallas_call(
        prepare_kernel,
        in_specs=[SCALARS, pl.BlockSpec(memory_space=pl.ANY), WHOLE],
        out_specs=WHOLE,
        out_shape=jax.ShapeDtypeStruct((2, 3, 2, 256, edges), jnp.bfloat16),
        compiler_params=limit(4),
        cost_estimate=pl.CostEstimate(flops=10_000_000, bytes_accessed=8_000_000, transcendentals=0),
        name="prepare_fields",
    )(places, after, rx_field)


def gate_kernel(after0_ref, after1_ref, value_ref, o_ref):
    pass


def gate(after, value):
    anywhere = pl.BlockSpec(memory_space=pl.ANY)
    return pl.pallas_call(
        gate_kernel,
        in_specs=[anywhere] * 3,
        out_specs=anywhere,
        out_shape=jax.ShapeDtypeStruct(value.shape, value.dtype),
        input_output_aliases={2: 0},
        compiler_params=limit(2),
        name="gate",
    )(*after, value)


def collect_kernel(own_ref, own_c_ref, flipped_ref, flipped_c_ref, o_ref):
    o_ref[...] = jnp.zeros_like(o_ref)
    for part in range(2):
        for g, value in enumerate((own_ref, own_c_ref, flipped_ref, flipped_c_ref)):
            o_ref[part, ROWS * g : ROWS * g + 100, :] = value[:, part, :]


def collect(*fields):
    return pl.pallas_call(
        collect_kernel,
        in_specs=[WHOLE] * 4,
        out_specs=WHOLE,
        out_shape=jax.ShapeDtypeStruct((2, 4 * ROWS, fields[0].shape[2]), jnp.float32),
        compiler_params=limit(4),
        name="collect",
    )(*fields)


def lane_group():
    return lax.broadcasted_iota(jnp.int32, (ROWS, 128), 1) // 32


def product_kernel(half, sources, index_ref, *refs):
    blocks, (tx, field, before, o_ref, w_scr, wh_scr, wl_scr) = refs[:-7], refs[-7:]
    tx_index = index_ref[0]
    group = lane_group()
    for part in range(2):
        for s in range(2):
            rolled = []
            for k, (ref, place) in enumerate(sources[s]):
                block = blocks[ref][part] if place is None else blocks[ref][place, part]
                rolled.append(pltpu.roll(block, 32 * k, 1) if k else block)
            for g in range(4):
                mixed = rolled[(0 - g) % 4]
                for lane in range(1, 4):
                    mixed = jnp.where(group == lane, rolled[(lane - g) % 4], mixed)
                if g:
                    mixed = pltpu.roll(mixed, 128 - 32 * g, 1)
                row = pl.multiple_of(jnp.bitwise_xor(tx_index, g) * ROWS, 8)
                w_scr[part, pl.ds(row, ROWS), 128 * s : 128 * (s + 1)] = mixed
    real, imag = w_scr[0], w_scr[1]
    for n, value in enumerate((real + imag, real, imag)):
        high, low = split(value)
        wh_scr[n, :, 0:256] = high
        wh_scr[n, :, 256:512] = high
        wl_scr[n] = low
    for tile in range(field.shape[4] // 256):
        cols = slice(256 * tile, 256 * (tile + 1))
        products = []
        for n in range(3):
            both = field[half, n, :, :, cols].reshape(512, 256)
            high = field[half, n, 1, :, cols]
            products.append(
                jnp.dot(wh_scr[n], both, preferred_element_type=jnp.float32)
                + jnp.dot(wl_scr[n], high, preferred_element_type=jnp.float32)
            )
        a, b = tx[0, :, cols], tx[1, :, cols]
        term = (a - b) * products[0] - b * products[1] - a * products[2]
        o_ref[:, cols] = before[:, cols] + jnp.sum(term, axis=0, keepdims=True)


def product(half, sources, index, blocks, tx, fields, before):
    edges = fields.shape[4]
    return pl.pallas_call(
        functools.partial(product_kernel, half, sources),
        in_specs=[SCALARS] + [WHOLE] * (len(blocks) + 3),
        out_specs=WHOLE,
        scratch_shapes=[
            pltpu.VMEM((2, 4 * ROWS, 256), jnp.float32),
            pltpu.VMEM((3, 4 * ROWS, 512), jnp.bfloat16),
            pltpu.VMEM((3, 4 * ROWS, 256), jnp.bfloat16),
        ],
        out_shape=jax.ShapeDtypeStruct((1, edges), jnp.float32),
        compiler_params=limit(12),
        cost_estimate=pl.CostEstimate(flops=3_000_000_000, bytes_accessed=6_000_000, transcendentals=0),
        name="product",
    )(index, *blocks, tx, fields, before)


def onehot_kernel(index_ref, cells_ref, component_ref, hot_ref, row_ref):
    x_lo, core, base = index_ref[1], index_ref[2], index_ref[3]
    cells = cells_ref[...] - base
    edges = cells.shape[1]
    lanes = lax.broadcasted_iota(jnp.int32, (128, edges), 0)
    for j in range(4):
        hit = lanes == jnp.bitwise_and(cells[j : j + 1, :], 127)
        hot_ref[j] = jnp.where(hit, 1.0, 0.0).astype(jnp.bfloat16)
    block = cells >> 7
    row = component_ref[...] * 3
    other = 8 * core + 2 * x_lo
    row_ref[...] = jnp.where(
        block == 4 + 2 * x_lo + core,
        row,
        jnp.where(block == other + core, row + 1, jnp.where(block == other + 1 - core, row + 2, -1)),
    )


def onehots(index, incidence, component):
    edges = incidence.shape[0]
    return pl.pallas_call(
        onehot_kernel,
        in_specs=[SCALARS, WHOLE, WHOLE],
        out_specs=(WHOLE, WHOLE),
        compiler_params=limit(2),
        out_shape=(
            jax.ShapeDtypeStruct((4, 128, edges), jnp.bfloat16),
            jax.ShapeDtypeStruct((4, edges), jnp.int32),
        ),
        name="onehots",
    )(index, incidence.T, component[None, :])


def scatter_kernel(e0, e1, e2, e3, hot_ref, row_ref, own_ref, send_ref):
    total = 0.25 * ((e0[...] + e1[...]) + (e2[...] + e3[...]))
    edges = total.shape[1]
    rows = lax.broadcasted_iota(jnp.int32, (16, edges), 0)
    first = total.astype(jnp.bfloat16).astype(jnp.float32)
    rest = total - first
    second = rest.astype(jnp.bfloat16).astype(jnp.float32)
    third = rest - second
    summed = jnp.zeros((48, 128), jnp.float32)
    for j in range(4):
        hit = rows == row_ref[j : j + 1, :]
        left = jnp.concatenate([jnp.where(hit, v, 0.0) for v in (first, second, third)], axis=0)
        summed += lax.dot_general(
            left.astype(jnp.bfloat16), hot_ref[j], (((1,), (1,)), ((), ())), preferred_element_type=jnp.float32
        )
    cells = (summed[0:16] + summed[16:32]) + summed[32:48]
    for k in range(3):
        own_ref[k : k + 1, :] = cells[3 * k : 3 * k + 1, :]
        send_ref[0, k : k + 1, :] = cells[3 * k + 1 : 3 * k + 2, :]
        send_ref[1, k : k + 1, :] = cells[3 * k + 2 : 3 * k + 3, :]


def scatter(terms, hot, row):
    return pl.pallas_call(
        scatter_kernel,
        in_specs=[WHOLE] * 6,
        out_specs=(WHOLE, WHOLE),
        compiler_params=limit(4),
        out_shape=(jax.ShapeDtypeStruct((3, 128), jnp.float32), jax.ShapeDtypeStruct((2, 3, 128), jnp.float32)),
        name="scatter_cells",
    )(*terms, hot, row)


def total_kernel(own_ref, received_ref, passed_ref, o_ref):
    o_ref[...] = own_ref[...] + received_ref[0] + passed_ref[...]


def total(own, received, passed):
    return pl.pallas_call(
        total_kernel,
        in_specs=[WHOLE] * 3,
        out_specs=WHOLE,
        compiler_params=limit(2),
        out_shape=jax.ShapeDtypeStruct(own.shape, jnp.float32),
        name="total",
    )(own, received, passed)


def neighbour_parts(block):
    route = []
    for m in range(64):
        for j in range(4):
            source = m + 1 if j % 2 == 0 else m - 1
            if 0 <= source < 64:
                route.append((source * 4 + j, m * 4 + j))
    return lax.ppermute(block, AXES, route)


def flip_x(x_hi, z, y, x_lo, core):
    return x_hi, z, y, 1 - x_lo, core


def flip_core(x_hi, z, y, x_lo, core):
    return x_hi, z, y, x_lo, 1 - core


def flip_both(x_hi, z, y, x_lo, core):
    return x_hi, z, y, 1 - x_lo, 1 - core


def z_source(turn):
    return lambda x_hi, z, y, x_lo, core: (
        x_lo,
        4 * core + ((z % 4) ^ turn),
        y,
        x_hi,
        1 - core if z // 4 == core else core,
    )


def y_partner(pairs, y):
    return (y ^ 1) if pairs == 0 else (y + 2 * (y % 2) - 1) % SIZE_Y


def y_source(pairs):
    return lambda x_hi, z, y, x_lo, core: (x_hi, z, y_partner(pairs, y), x_lo, core)


def shards(tx_field, rx_field, misfit_weight, incidence, component):
    mesh_index = lax.axis_index("mesh")
    tx_index = lax.axis_index("tx")
    z, y = (mesh_index // 4) % 8, mesh_index % 4
    packed = pack_weight(misfit_weight)
    tx_own = tx_field.transpose(1, 0, 2)
    tx_x = fetch(tx_own, flip_x)
    from_z = [fetch(packed, z_source(turn)) for turn in TURNS]
    y_places = [y, y_partner(0, y), y_partner(1, y), (y + 2) % SIZE_Y]
    places = jnp.stack([(z % 4) ^ turn for turn in TURNS] + y_places).astype(jnp.int32)
    index = jnp.stack([tx_index, tx_index // 2, tx_index % 2, (mesh_index - 1) * CELL_TILE]).astype(jnp.int32)
    hot, row = onehots(index, incidence, component)

    stacked = [jnp.stack(from_z[2 * g : 2 * g + 2]) for g in range(2)]
    tx_c = fetch(tx_own, flip_core)
    tx_x = gate(stacked, tx_x)
    tx_xc = fetch(tx_x, flip_core)
    near = [fetch(stacked[g], y_source(0)) for g in range(2)]
    far = [fetch(stacked[g], y_source(1)) for g in range(2)]
    last = [fetch(near[0], y_source(1)), fetch(far[1], y_source(0))]
    fields = prepare_fields(places, stacked[1], rx_field)
    tx = collect(tx_own, tx_c, tx_x, tx_xc)
    edge = jnp.zeros((1, tx_field.shape[2]), jnp.float32)
    early = [[(k, None) for k in range(4)], [(4, 0), (4, 1), (5, 0), (5, 1)]]
    late = [[(0, 0), (0, 1), (1, 0), (1, 1)], [(2, 0), (2, 1), (3, 0), (3, 1)]]
    edge = product(0, early, index, from_z + near, tx, fields, edge)
    edge = product(1, late, index, far + last, tx, fields, edge)
    terms = [edge, fetch(edge, flip_core), fetch(edge, flip_x), fetch(edge, flip_both)]
    own, send = scatter(terms, hot, row)
    received = neighbour_parts(send)
    return total(own, received, fetch(received[1], flip_core))


def solution(mesh):
    return jax.shard_map(
        shards,
        mesh=mesh,
        in_specs=(
            P(None, "tx", "mesh"),
            P(None, "tx", "mesh"),
            P(None, None, "mesh"),
            P("mesh", None),
            P("mesh"),
        ),
        out_specs=P(None, ("mesh", "tx")),
        check_vma=False,
    )
```

```python
import functools

import jax
import jax.numpy as jnp
from jax import lax
from jax.experimental import pallas as pl
from jax.experimental.pallas import tpu as pltpu
from jax.sharding import PartitionSpec as P

CELL_TILE = 512
AXES = ("mesh", "tx")
SIZE_Z, SIZE_Y = 8, 4
TURNS = (3, 2, 1, 0)
ROWS = 104
MIB = 1024 * 1024
WHOLE = pl.BlockSpec(memory_space=pltpu.VMEM)
SCALARS = pl.BlockSpec(memory_space=pltpu.SMEM)


def limit(mib):
    return pltpu.CompilerParams(vmem_limit_bytes=mib * MIB)


def coords(device):
    mesh_index, tx_index = divmod(device, 4)
    return mesh_index // 32, (mesh_index // 4) % 8, mesh_index % 4, tx_index // 2, tx_index % 2


def device_at(x_hi, z, y, x_lo, core):
    return ((x_hi % 2) * 32 + (z % 8) * 4 + y % 4) * 4 + (x_lo % 2) * 2 + core % 2


def fetch(block, source_of):
    route = [(device_at(*source_of(*coords(d))), d) for d in range(256)]
    return lax.ppermute(block, AXES, route)


def pack_kernel(w_ref, o_ref):
    for part in range(2):
        value = w_ref[part].T
        pieces = [value[100 * g : 100 * (g + 1), :] for g in range(4)]
        o_ref[100 * part : 100 * (part + 1), :] = jnp.concatenate(pieces, axis=1)


def pack_weight(misfit_weight):
    return pl.pallas_call(
        pack_kernel,
        in_specs=[WHOLE],
        out_specs=WHOLE,
        out_shape=jax.ShapeDtypeStruct((200, 128), jnp.float32),
        compiler_params=limit(2),
        name="pack_weight",
    )(misfit_weight.transpose(0, 2, 1))


def split(value):
    high = value.astype(jnp.bfloat16)
    low = (value - high.astype(jnp.float32)).astype(jnp.bfloat16)
    return high, low


def prepare_kernel(place_ref, after_ref, rx_ref, early_ref, late_ref):
    for s in range(4):
        for k in range(4):
            row = pl.multiple_of(place_ref[k] * 128 + place_ref[4 + s] * 32, 32)
            real, imag = rx_ref[0, pl.ds(row, 32), :], rx_ref[1, pl.ds(row, 32), :]
            out, first = (early_ref, 128 * s) if s < 2 else (late_ref, 128 * (s - 2))
            rows = slice(first + 32 * k, first + 32 * (k + 1))
            for n, value in enumerate((real, imag - real, real + imag)):
                high, low = split(value)
                out[n, 0, rows, :] = low
                out[n, 1, rows, :] = high


def prepare_fields(places, after, rx_field):
    edges = rx_field.shape[2]
    return pl.pallas_call(
        prepare_kernel,
        in_specs=[SCALARS, pl.BlockSpec(memory_space=pl.ANY), WHOLE],
        out_specs=(WHOLE, WHOLE),
        out_shape=tuple(jax.ShapeDtypeStruct((3, 2, rows, edges), jnp.bfloat16) for rows in (256, 256)),
        compiler_params=limit(4),
        cost_estimate=pl.CostEstimate(flops=10_000_000, bytes_accessed=8_000_000, transcendentals=0),
        name="prepare_fields",
    )(places, after, rx_field)


def gate_kernel(after0_ref, after1_ref, value_ref, o_ref):
    pass


def gate(after, value):
    anywhere = pl.BlockSpec(memory_space=pl.ANY)
    return pl.pallas_call(
        gate_kernel,
        in_specs=[anywhere] * 3,
        out_specs=anywhere,
        out_shape=jax.ShapeDtypeStruct(value.shape, value.dtype),
        input_output_aliases={2: 0},
        compiler_params=limit(2),
        name="gate",
    )(*after, value)


def collect_kernel(own_ref, own_c_ref, flipped_ref, flipped_c_ref, o_ref):
    o_ref[...] = jnp.zeros_like(o_ref)
    for part in range(2):
        for g, value in enumerate((own_ref, own_c_ref, flipped_ref, flipped_c_ref)):
            o_ref[part, ROWS * g : ROWS * g + 100, :] = value[:, part, :]


def collect(*fields):
    return pl.pallas_call(
        collect_kernel,
        in_specs=[WHOLE] * 4,
        out_specs=WHOLE,
        out_shape=jax.ShapeDtypeStruct((2, 4 * ROWS, fields[0].shape[2]), jnp.float32),
        compiler_params=limit(4),
        name="collect",
    )(*fields)


def lane_group():
    return lax.broadcasted_iota(jnp.int32, (100, 128), 1) // 32


def product_kernel(sources, index_ref, *refs):
    blocks, (tx, field, before, o_ref, w_scr, wh_scr, wl_scr) = refs[:-7], refs[-7:]
    tx_index = index_ref[0]
    group = lane_group()
    for g in range(4):
        w_scr[:, ROWS * g + 100 : ROWS * (g + 1), :] = jnp.zeros((2, ROWS - 100, w_scr.shape[2]), jnp.float32)
    for part in range(2):
        for s in range(len(sources)):
            rolled = []
            for k, (ref, place) in enumerate(sources[s]):
                rows = pl.ds(100 * part, 100)
                block = blocks[ref][rows, :] if place is None else blocks[ref][place, rows, :]
                rolled.append(pltpu.roll(block, 32 * k, 1) if k else block)
            for g in range(4):
                mixed = rolled[(0 - g) % 4]
                for lane in range(1, 4):
                    mixed = jnp.where(group == lane, rolled[(lane - g) % 4], mixed)
                if g:
                    mixed = pltpu.roll(mixed, 128 - 32 * g, 1)
                row = pl.multiple_of(jnp.bitwise_xor(tx_index, g) * ROWS, 8)
                w_scr[part, pl.ds(row, 100), 128 * s : 128 * (s + 1)] = mixed
    depth = 128 * len(sources)
    real, imag = w_scr[0], w_scr[1]
    for n, value in enumerate((real + imag, real, imag)):
        high, low = split(value)
        wh_scr[n, :, 0:depth] = high
        wh_scr[n, :, depth:] = high
        wl_scr[n] = low
    for tile in range(field.shape[3] // 256):
        cols = slice(256 * tile, 256 * (tile + 1))
        products = []
        for n in range(3):
            both = field[n, :, :, cols].reshape(2 * depth, 256)
            high = field[n, 1, :, cols]
            products.append(
                jnp.dot(wh_scr[n], both, preferred_element_type=jnp.float32)
                + jnp.dot(wl_scr[n], high, preferred_element_type=jnp.float32)
            )
        a, b = tx[0, :, cols], tx[1, :, cols]
        term = (a - b) * products[0] - b * products[1] - a * products[2]
        o_ref[:, cols] = before[:, cols] + jnp.sum(term, axis=0, keepdims=True)


def product(sources, index, blocks, tx, fields, before):
    edges, depth = fields.shape[3], fields.shape[2]
    return pl.pallas_call(
        functools.partial(product_kernel, sources),
        in_specs=[SCALARS] + [WHOLE] * (len(blocks) + 3),
        out_specs=WHOLE,
        scratch_shapes=[
            pltpu.VMEM((2, 4 * ROWS, depth), jnp.float32),
            pltpu.VMEM((3, 4 * ROWS, 2 * depth), jnp.bfloat16),
            pltpu.VMEM((3, 4 * ROWS, depth), jnp.bfloat16),
        ],
        out_shape=jax.ShapeDtypeStruct((1, edges), jnp.float32),
        compiler_params=limit(12),
        cost_estimate=pl.CostEstimate(flops=3_000_000_000, bytes_accessed=6_000_000, transcendentals=0),
        name="product",
    )(index, *blocks, tx, fields, before)


def onehot_kernel(index_ref, cells_ref, component_ref, hot_ref, row_ref):
    x_lo, core, base, send_x_lo = index_ref[1], index_ref[2], index_ref[3], index_ref[4]
    cells = cells_ref[...] - base
    edges = cells.shape[1]
    lanes = lax.broadcasted_iota(jnp.int32, (128, edges), 0)
    for j in range(4):
        hit = lanes == jnp.bitwise_and(cells[j : j + 1, :], 127)
        hot_ref[j] = jnp.where(hit, 1.0, 0.0).astype(jnp.bfloat16)
    block = cells >> 7
    row = component_ref[...] * 3
    other = 8 * core + 2 * send_x_lo
    row_ref[...] = jnp.where(
        block == 4 + 2 * x_lo + core,
        row,
        jnp.where(block == other + core, row + 1, jnp.where(block == other + 1 - core, row + 2, -1)),
    )


def onehots(index, incidence, component):
    edges = incidence.shape[0]
    return pl.pallas_call(
        onehot_kernel,
        in_specs=[SCALARS, WHOLE, WHOLE],
        out_specs=(WHOLE, WHOLE),
        compiler_params=limit(2),
        out_shape=(
            jax.ShapeDtypeStruct((4, 128, edges), jnp.bfloat16),
            jax.ShapeDtypeStruct((4, edges), jnp.int32),
        ),
        name="onehots",
    )(index, incidence.T, component[None, :])


def scatter_kernel(e0, e1, e2, e3, hot_ref, row_ref, own_ref, send_ref):
    total = 0.25 * ((e0[...] + e1[...]) + (e2[...] + e3[...]))
    edges = total.shape[1]
    rows = lax.broadcasted_iota(jnp.int32, (16, edges), 0)
    first = total.astype(jnp.bfloat16).astype(jnp.float32)
    rest = total - first
    second = rest.astype(jnp.bfloat16).astype(jnp.float32)
    third = rest - second
    summed = jnp.zeros((48, 128), jnp.float32)
    for j in range(4):
        hit = rows == row_ref[j : j + 1, :]
        left = jnp.concatenate([jnp.where(hit, v, 0.0) for v in (first, second, third)], axis=0)
        summed += lax.dot_general(
            left.astype(jnp.bfloat16), hot_ref[j], (((1,), (1,)), ((), ())), preferred_element_type=jnp.float32
        )
    cells = (summed[0:16] + summed[16:32]) + summed[32:48]
    for k in range(3):
        own_ref[k : k + 1, :] = cells[3 * k : 3 * k + 1, :]
        send_ref[0, k : k + 1, :] = cells[3 * k + 1 : 3 * k + 2, :]
        send_ref[1, k : k + 1, :] = cells[3 * k + 2 : 3 * k + 3, :]


def scatter(terms, hot, row):
    return pl.pallas_call(
        scatter_kernel,
        in_specs=[WHOLE] * 6,
        out_specs=(WHOLE, WHOLE),
        compiler_params=limit(4),
        out_shape=(jax.ShapeDtypeStruct((3, 128), jnp.float32), jax.ShapeDtypeStruct((2, 3, 128), jnp.float32)),
        name="scatter_cells",
    )(*terms, hot, row)


def total_kernel(own_ref, received_ref, passed_ref, o_ref):
    o_ref[...] = own_ref[...] + received_ref[0] + passed_ref[...]


def total(own, received, passed):
    return pl.pallas_call(
        total_kernel,
        in_specs=[WHOLE] * 3,
        out_specs=WHOLE,
        compiler_params=limit(2),
        out_shape=jax.ShapeDtypeStruct(own.shape, jnp.float32),
        name="total",
    )(own, received, passed)


def neighbour_parts(block):
    route = []
    for m in range(64):
        for j in range(4):
            source = m + 1 if j % 2 == 0 else m - 1
            flip = 2 if {m, source} == {31, 32} else 0
            if 0 <= source < 64:
                route.append((source * 4 + (j ^ flip), m * 4 + j))
    return lax.ppermute(block, AXES, route)


def flip_x(x_hi, z, y, x_lo, core):
    return x_hi, z, y, 1 - x_lo, core


def flip_core(x_hi, z, y, x_lo, core):
    return x_hi, z, y, x_lo, 1 - core


def flip_both(x_hi, z, y, x_lo, core):
    return x_hi, z, y, 1 - x_lo, 1 - core


def z_source(turn):
    return lambda x_hi, z, y, x_lo, core: (
        x_lo,
        4 * core + ((z % 4) ^ turn),
        y,
        x_hi,
        1 - core if z // 4 == core else core,
    )


def y_partner(pairs, y):
    return (y ^ 1) if pairs == 0 else (y + 2 * (y % 2) - 1) % SIZE_Y


def y_source(pairs):
    return lambda x_hi, z, y, x_lo, core: (x_hi, z, y_partner(pairs, y), x_lo, core)


def shards(tx_field, rx_field, misfit_weight, incidence, component):
    mesh_index = lax.axis_index("mesh")
    tx_index = lax.axis_index("tx")
    z, y = (mesh_index // 4) % 8, mesh_index % 4
    packed = pack_weight(misfit_weight)
    tx_own = tx_field.transpose(1, 0, 2)
    tx_x = fetch(tx_own, flip_x)
    from_z = [fetch(packed, z_source(turn)) for turn in TURNS]
    y_places = [y, y_partner(0, y), y_partner(1, y), (y + 2) % SIZE_Y]
    places = jnp.stack([(z % 4) ^ turn for turn in TURNS] + y_places).astype(jnp.int32)
    x_lo, core = tx_index // 2, tx_index % 2
    flipped = mesh_index == jnp.where(core == 0, 32, 31)
    send_x_lo = jnp.where(flipped, 1 - x_lo, x_lo)
    index = jnp.stack([tx_index, x_lo, core, (mesh_index - 1) * CELL_TILE, send_x_lo]).astype(jnp.int32)
    hot, row = onehots(index, incidence, component)

    stacked = [jnp.stack(from_z[2 * g : 2 * g + 2]) for g in range(2)]
    tx_c = fetch(tx_own, flip_core)
    tx_x = gate(stacked, tx_x)
    tx_xc = fetch(tx_x, flip_core)
    near = [fetch(stacked[g], y_source(0)) for g in range(2)]
    far = [fetch(stacked[g], y_source(1)) for g in range(2)]
    last = [fetch(near[0], y_source(1)), fetch(far[1], y_source(0))]
    fields = prepare_fields(places, stacked[1], rx_field)
    tx = collect(tx_own, tx_c, tx_x, tx_xc)
    edge = jnp.zeros((1, tx_field.shape[2]), jnp.float32)
    pairs = lambda first: [(first, 0), (first, 1), (first + 1, 0), (first + 1, 1)]
    early = [[(k, None) for k in range(4)], pairs(4)]
    edge = product(early, index, from_z + near, tx, fields[0], edge)
    edge = product([pairs(0), pairs(2)], index, far + last, tx, fields[1], edge)
    terms = [edge, fetch(edge, flip_core), fetch(edge, flip_x), fetch(edge, flip_both)]
    own, send = scatter(terms, hot, row)
    received = neighbour_parts(send)
    return total(own, received, fetch(received[1], flip_core))


def solution(mesh):
    return jax.shard_map(
        shards,
        mesh=mesh,
        in_specs=(
            P(None, "tx", "mesh"),
            P(None, "tx", "mesh"),
            P(None, None, "mesh"),
            P("mesh", None),
            P("mesh"),
        ),
        out_specs=P(None, ("mesh", "tx")),
        check_vma=False,
    )
```

```python
import functools

import jax
import jax.numpy as jnp
from jax import lax
from jax.experimental import pallas as pl
from jax.experimental.pallas import tpu as pltpu
from jax.sharding import PartitionSpec as P

CELL_TILE = 512
AXES = ("mesh", "tx")
SIZE_Z, SIZE_Y = 8, 4
FAR_TURNS = (3, 2, 0, 1)
NEAR_TURNS = (3, 2, 0, 1)
ROWS = 104
MIB = 1024 * 1024
WHOLE = pl.BlockSpec(memory_space=pltpu.VMEM)
SCALARS = pl.BlockSpec(memory_space=pltpu.SMEM)


def limit(mib):
    return pltpu.CompilerParams(vmem_limit_bytes=mib * MIB)


def coords(device):
    mesh_index, tx_index = divmod(device, 4)
    return mesh_index // 32, (mesh_index // 4) % 8, mesh_index % 4, tx_index // 2, tx_index % 2


def device_at(x_hi, z, y, x_lo, core):
    return ((x_hi % 2) * 32 + (z % 8) * 4 + y % 4) * 4 + (x_lo % 2) * 2 + core % 2


def fetch(block, source_of):
    route = [(device_at(*source_of(*coords(d))), d) for d in range(256)]
    return lax.ppermute(block, AXES, route)


def pack_kernel(w_ref, o_ref):
    for part in range(2):
        value = w_ref[part].T
        pieces = [value[100 * g : 100 * (g + 1), :] for g in range(4)]
        o_ref[100 * part : 100 * (part + 1), :] = jnp.concatenate(pieces, axis=1)


def pack_weight(misfit_weight):
    return pl.pallas_call(
        pack_kernel,
        in_specs=[WHOLE],
        out_specs=WHOLE,
        out_shape=jax.ShapeDtypeStruct((200, 128), jnp.float32),
        compiler_params=limit(2),
        name="pack_weight",
    )(misfit_weight.transpose(0, 2, 1))


def split(value):
    high = value.astype(jnp.bfloat16)
    low = (value - high.astype(jnp.float32)).astype(jnp.bfloat16)
    return high, low


def prepare_kernel(place_ref, rx_ref, early_ref, late_ref):
    for s in range(4):
        for k in range(4):
            turned = 3 - s if s in (1, 2) and k >= 2 else s
            row = pl.multiple_of(place_ref[k] * 128 + place_ref[4 + turned] * 32, 32)
            real, imag = rx_ref[0, pl.ds(row, 32), :], rx_ref[1, pl.ds(row, 32), :]
            out, first = (early_ref, 128 * s) if s < 2 else (late_ref, 128 * (s - 2))
            rows = slice(first + 32 * k, first + 32 * (k + 1))
            for n, value in enumerate((real, imag - real, real + imag)):
                high, low = split(value)
                out[n, 0, rows, :] = low
                out[n, 1, rows, :] = high


def prepare_fields(places, rx_field):
    edges = rx_field.shape[2]
    return pl.pallas_call(
        prepare_kernel,
        in_specs=[SCALARS, WHOLE],
        out_specs=(WHOLE, WHOLE),
        out_shape=tuple(jax.ShapeDtypeStruct((3, 2, rows, edges), jnp.bfloat16) for rows in (256, 256)),
        compiler_params=limit(4),
        cost_estimate=pl.CostEstimate(flops=10_000_000, bytes_accessed=8_000_000, transcendentals=0),
        name="prepare_fields",
    )(places, rx_field)


def gate_kernel(*refs):
    pass


def gate(after, value):
    anywhere = pl.BlockSpec(memory_space=pl.ANY)
    return pl.pallas_call(
        gate_kernel,
        in_specs=[anywhere] * (len(after) + 1),
        out_specs=anywhere,
        out_shape=jax.ShapeDtypeStruct(value.shape, value.dtype),
        input_output_aliases={len(after): 0},
        compiler_params=limit(2),
        name="gate",
    )(*after, value)


def collect_kernel(own_ref, own_c_ref, flipped_ref, flipped_c_ref, o_ref):
    o_ref[...] = jnp.zeros_like(o_ref)
    for part in range(2):
        for g, value in enumerate((own_ref, own_c_ref, flipped_ref, flipped_c_ref)):
            o_ref[part, ROWS * g : ROWS * g + 100, :] = value[:, part, :]


def collect(*fields):
    return pl.pallas_call(
        collect_kernel,
        in_specs=[WHOLE] * 4,
        out_specs=WHOLE,
        out_shape=jax.ShapeDtypeStruct((2, 4 * ROWS, fields[0].shape[2]), jnp.float32),
        compiler_params=limit(4),
        name="collect",
    )(*fields)


def lane_group():
    return lax.broadcasted_iota(jnp.int32, (100, 128), 1) // 32


def product_kernel(sources, index_ref, *refs):
    blocks, (tx, field, before, o_ref, w_scr, wh_scr, wl_scr) = refs[:-7], refs[-7:]
    tx_index = index_ref[0]
    group = lane_group()
    for g in range(4):
        w_scr[:, ROWS * g + 100 : ROWS * (g + 1), :] = jnp.zeros((2, ROWS - 100, w_scr.shape[2]), jnp.float32)
    for part in range(2):
        for s in range(len(sources)):
            rolled = []
            for k, (ref, place) in enumerate(sources[s]):
                rows = pl.ds(100 * part, 100)
                block = blocks[ref][rows, :] if place is None else blocks[ref][place, rows, :]
                rolled.append(pltpu.roll(block, 32 * k, 1) if k else block)
            for g in range(4):
                mixed = rolled[(0 - g) % 4]
                for lane in range(1, 4):
                    mixed = jnp.where(group == lane, rolled[(lane - g) % 4], mixed)
                if g:
                    mixed = pltpu.roll(mixed, 128 - 32 * g, 1)
                row = pl.multiple_of(jnp.bitwise_xor(tx_index, g) * ROWS, 8)
                w_scr[part, pl.ds(row, 100), 128 * s : 128 * (s + 1)] = mixed
    depth = 128 * len(sources)
    real, imag = w_scr[0], w_scr[1]
    for n, value in enumerate((real + imag, real, imag)):
        high, low = split(value)
        wh_scr[n, :, 0:depth] = high
        wh_scr[n, :, depth:] = high
        wl_scr[n] = low
    for tile in range(field.shape[3] // 256):
        cols = slice(256 * tile, 256 * (tile + 1))
        products = []
        for n in range(3):
            both = field[n, :, :, cols].reshape(2 * depth, 256)
            high = field[n, 1, :, cols]
            products.append(
                jnp.dot(wh_scr[n], both, preferred_element_type=jnp.float32)
                + jnp.dot(wl_scr[n], high, preferred_element_type=jnp.float32)
            )
        a, b = tx[0, :, cols], tx[1, :, cols]
        term = (a - b) * products[0] - b * products[1] - a * products[2]
        o_ref[:, cols] = before[:, cols] + jnp.sum(term, axis=0, keepdims=True)


def product(sources, index, blocks, tx, fields, before):
    edges, depth = fields.shape[3], fields.shape[2]
    return pl.pallas_call(
        functools.partial(product_kernel, sources),
        in_specs=[SCALARS] + [WHOLE] * (len(blocks) + 3),
        out_specs=WHOLE,
        scratch_shapes=[
            pltpu.VMEM((2, 4 * ROWS, depth), jnp.float32),
            pltpu.VMEM((3, 4 * ROWS, 2 * depth), jnp.bfloat16),
            pltpu.VMEM((3, 4 * ROWS, depth), jnp.bfloat16),
        ],
        out_shape=jax.ShapeDtypeStruct((1, edges), jnp.float32),
        compiler_params=limit(12),
        cost_estimate=pl.CostEstimate(flops=3_000_000_000, bytes_accessed=6_000_000, transcendentals=0),
        name="product",
    )(index, *blocks, tx, fields, before)


def onehot_kernel(index_ref, cells_ref, component_ref, hot_ref, row_ref):
    x_lo, core, base, send_x_lo = index_ref[1], index_ref[2], index_ref[3], index_ref[4]
    cells = cells_ref[...] - base
    edges = cells.shape[1]
    lanes = lax.broadcasted_iota(jnp.int32, (128, edges), 0)
    for j in range(4):
        hit = lanes == jnp.bitwise_and(cells[j : j + 1, :], 127)
        hot_ref[j] = jnp.where(hit, 1.0, 0.0).astype(jnp.bfloat16)
    block = cells >> 7
    row = component_ref[...] * 3
    other = 8 * core + 2 * send_x_lo
    row_ref[...] = jnp.where(
        block == 4 + 2 * x_lo + core,
        row,
        jnp.where(block == other + core, row + 1, jnp.where(block == other + 1 - core, row + 2, -1)),
    )


def onehots(index, incidence, component):
    edges = incidence.shape[0]
    return pl.pallas_call(
        onehot_kernel,
        in_specs=[SCALARS, WHOLE, WHOLE],
        out_specs=(WHOLE, WHOLE),
        compiler_params=limit(2),
        out_shape=(
            jax.ShapeDtypeStruct((4, 128, edges), jnp.bfloat16),
            jax.ShapeDtypeStruct((4, edges), jnp.int32),
        ),
        name="onehots",
    )(index, incidence.T, component[None, :])


def scatter_kernel(e0, e1, e2, e3, hot_ref, row_ref, own_ref, send_ref):
    total = 0.25 * ((e0[...] + e1[...]) + (e2[...] + e3[...]))
    edges = total.shape[1]
    rows = lax.broadcasted_iota(jnp.int32, (16, edges), 0)
    first = total.astype(jnp.bfloat16).astype(jnp.float32)
    rest = total - first
    second = rest.astype(jnp.bfloat16).astype(jnp.float32)
    third = rest - second
    summed = jnp.zeros((48, 128), jnp.float32)
    for j in range(4):
        hit = rows == row_ref[j : j + 1, :]
        left = jnp.concatenate([jnp.where(hit, v, 0.0) for v in (first, second, third)], axis=0)
        summed += lax.dot_general(
            left.astype(jnp.bfloat16), hot_ref[j], (((1,), (1,)), ((), ())), preferred_element_type=jnp.float32
        )
    cells = (summed[0:16] + summed[16:32]) + summed[32:48]
    for k in range(3):
        own_ref[k : k + 1, :] = cells[3 * k : 3 * k + 1, :]
        send_ref[0, k : k + 1, :] = cells[3 * k + 1 : 3 * k + 2, :]
        send_ref[1, k : k + 1, :] = cells[3 * k + 2 : 3 * k + 3, :]


def scatter(terms, hot, row):
    return pl.pallas_call(
        scatter_kernel,
        in_specs=[WHOLE] * 6,
        out_specs=(WHOLE, WHOLE),
        compiler_params=limit(4),
        out_shape=(jax.ShapeDtypeStruct((3, 128), jnp.float32), jax.ShapeDtypeStruct((2, 3, 128), jnp.float32)),
        name="scatter_cells",
    )(*terms, hot, row)


def total_kernel(own_ref, received_ref, passed_ref, o_ref):
    o_ref[...] = own_ref[...] + received_ref[0] + passed_ref[...]


def total(own, received, passed):
    return pl.pallas_call(
        total_kernel,
        in_specs=[WHOLE] * 3,
        out_specs=WHOLE,
        compiler_params=limit(2),
        out_shape=jax.ShapeDtypeStruct(own.shape, jnp.float32),
        name="total",
    )(own, received, passed)


def neighbour_parts(block):
    route = []
    for m in range(64):
        for j in range(4):
            source = m + 1 if j % 2 == 0 else m - 1
            flip = 2 if {m, source} == {31, 32} else 0
            if 0 <= source < 64:
                route.append((source * 4 + (j ^ flip), m * 4 + j))
    return lax.ppermute(block, AXES, route)


def flip_x(x_hi, z, y, x_lo, core):
    return x_hi, z, y, 1 - x_lo, core


def flip_core(x_hi, z, y, x_lo, core):
    return x_hi, z, y, x_lo, 1 - core


def flip_both(x_hi, z, y, x_lo, core):
    return x_hi, z, y, 1 - x_lo, 1 - core


def z_source(k):
    def source(x_hi, z, y, x_lo, core):
        if z // 4 == core:
            return x_lo, 4 * core + ((z % 4) ^ NEAR_TURNS[k]), y, x_hi, 1 - core
        return x_lo, 4 * core + ((z % 4) ^ FAR_TURNS[k]), y, x_hi, core

    return source


def y_partner(pairs, y):
    return (y ^ 1) if pairs == 0 else (y + 2 * (y % 2) - 1) % SIZE_Y


def y_source(pairs):
    return lambda x_hi, z, y, x_lo, core: (x_hi, z, y_partner(pairs, y), x_lo, core)


def shards(tx_field, rx_field, misfit_weight, incidence, component):
    mesh_index = lax.axis_index("mesh")
    tx_index = lax.axis_index("tx")
    z, y = (mesh_index // 4) % 8, mesh_index % 4
    packed = pack_weight(misfit_weight)
    tx_own = tx_field.transpose(1, 0, 2)
    tx_x = fetch(tx_own, flip_x)
    from_z = [fetch(packed, z_source(k)) for k in range(4)]
    y_places = [y, y_partner(0, y), y_partner(1, y), (y + 2) % SIZE_Y]
    same_half = z // 4 == tx_index % 2
    z_places = [(z % 4) ^ jnp.where(same_half, NEAR_TURNS[k], FAR_TURNS[k]) for k in range(4)]
    places = jnp.stack(z_places + y_places).astype(jnp.int32)
    x_lo, core = tx_index // 2, tx_index % 2
    flipped = mesh_index == jnp.where(core == 0, 32, 31)
    send_x_lo = jnp.where(flipped, 1 - x_lo, x_lo)
    index = jnp.stack([tx_index, x_lo, core, (mesh_index - 1) * CELL_TILE, send_x_lo]).astype(jnp.int32)
    hot, row = onehots(index, incidence, component)

    stacked = [jnp.stack(from_z[2 * g : 2 * g + 2]) for g in range(2)]
    tx_c = fetch(tx_own, flip_core)
    tx_x = gate(stacked, tx_x)
    tx_xc = fetch(tx_x, flip_core)
    near = [fetch(stacked[g], y_source(0)) for g in range(2)]
    far = [fetch(stacked[g], y_source(1)) for g in range(2)]
    last = [fetch(near[0], y_source(1)), fetch(far[1], y_source(0))]
    fields = prepare_fields(places, rx_field)
    tx = collect(tx_own, tx_c, tx_x, tx_xc)
    edge = jnp.zeros((1, tx_field.shape[2]), jnp.float32)
    pairs = lambda first: [(first, 0), (first, 1), (first + 1, 0), (first + 1, 1)]
    early = [[(k, None) for k in range(4)], pairs(4)]
    edge = product(early, index, from_z + [near[0], far[1]], tx, fields[0], edge)
    edge = product([pairs(0), pairs(2)], index, [far[0], near[1]] + last, tx, fields[1], edge)
    terms = [edge, fetch(edge, flip_core), fetch(edge, flip_x), fetch(edge, flip_both)]
    own, send = scatter(terms, hot, row)
    received = neighbour_parts(send)
    return total(own, received, fetch(received[1], flip_core))


def solution(mesh):
    return jax.shard_map(
        shards,
        mesh=mesh,
        in_specs=(
            P(None, "tx", "mesh"),
            P(None, "tx", "mesh"),
            P(None, None, "mesh"),
            P("mesh", None),
            P("mesh"),
        ),
        out_specs=P(None, ("mesh", "tx")),
        check_vma=False,
    )
```

```python
import functools

import jax
import jax.numpy as jnp
from jax import lax
from jax.experimental import pallas as pl
from jax.experimental.pallas import tpu as pltpu
from jax.sharding import PartitionSpec as P

CELL_TILE = 512
AXES = ("mesh", "tx")
SIZE_Z, SIZE_Y = 8, 4
FAR_TURNS = (3, 2, 0, 1)
NEAR_TURNS = (3, 2, 0, 1)
ROWS = 104
MIB = 1024 * 1024
WHOLE = pl.BlockSpec(memory_space=pltpu.VMEM)
SCALARS = pl.BlockSpec(memory_space=pltpu.SMEM)


def limit(mib):
    return pltpu.CompilerParams(vmem_limit_bytes=mib * MIB)


def coords(device):
    mesh_index, tx_index = divmod(device, 4)
    return mesh_index // 32, (mesh_index // 4) % 8, mesh_index % 4, tx_index // 2, tx_index % 2


def device_at(x_hi, z, y, x_lo, core):
    return ((x_hi % 2) * 32 + (z % 8) * 4 + y % 4) * 4 + (x_lo % 2) * 2 + core % 2


def fetch(block, source_of):
    route = [(device_at(*source_of(*coords(d))), d) for d in range(256)]
    return lax.ppermute(block, AXES, route)


def pack_kernel(w_ref, o_ref):
    for part in range(2):
        value = w_ref[part].T
        pieces = [value[100 * g : 100 * (g + 1), :] for g in range(4)]
        o_ref[100 * part : 100 * (part + 1), :] = jnp.concatenate(pieces, axis=1)


def pack_weight(misfit_weight):
    return pl.pallas_call(
        pack_kernel,
        in_specs=[WHOLE],
        out_specs=WHOLE,
        out_shape=jax.ShapeDtypeStruct((200, 128), jnp.float32),
        compiler_params=limit(2),
        name="pack_weight",
    )(misfit_weight.transpose(0, 2, 1))


def split(value):
    high = value.astype(jnp.bfloat16)
    low = (value - high.astype(jnp.float32)).astype(jnp.bfloat16)
    return high, low


def prepare_kernel(place_ref, rx_ref, early_ref, late_ref):
    for s in range(4):
        for k in range(4):
            turned = 3 - s if s in (1, 2) and k >= 2 else s
            row = pl.multiple_of(place_ref[k] * 128 + place_ref[4 + turned] * 32, 32)
            real, imag = rx_ref[0, pl.ds(row, 32), :], rx_ref[1, pl.ds(row, 32), :]
            out, first = (early_ref, 128 * s) if s < 2 else (late_ref, 128 * (s - 2))
            rows = slice(first + 32 * k, first + 32 * (k + 1))
            for n, value in enumerate((real, imag - real, real + imag)):
                high, low = split(value)
                out[n, 0, rows, :] = low
                out[n, 1, rows, :] = high


def prepare_fields(places, rx_field):
    edges = rx_field.shape[2]
    return pl.pallas_call(
        prepare_kernel,
        in_specs=[SCALARS, WHOLE],
        out_specs=(WHOLE, WHOLE),
        out_shape=tuple(jax.ShapeDtypeStruct((3, 2, rows, edges), jnp.bfloat16) for rows in (256, 256)),
        compiler_params=limit(4),
        cost_estimate=pl.CostEstimate(flops=10_000_000, bytes_accessed=8_000_000, transcendentals=0),
        name="prepare_fields",
    )(places, rx_field)


def gate_kernel(*refs):
    pass


def gate(after, value):
    anywhere = pl.BlockSpec(memory_space=pl.ANY)
    return pl.pallas_call(
        gate_kernel,
        in_specs=[anywhere] * (len(after) + 1),
        out_specs=anywhere,
        out_shape=jax.ShapeDtypeStruct(value.shape, value.dtype),
        input_output_aliases={len(after): 0},
        compiler_params=limit(2),
        name="gate",
    )(*after, value)


def collect_kernel(own_ref, own_c_ref, flipped_ref, flipped_c_ref, o_ref):
    o_ref[...] = jnp.zeros_like(o_ref)
    for part in range(2):
        for g, value in enumerate((own_ref, own_c_ref, flipped_ref, flipped_c_ref)):
            o_ref[part, ROWS * g : ROWS * g + 100, :] = value[:, part, :]


def collect(*fields):
    return pl.pallas_call(
        collect_kernel,
        in_specs=[WHOLE] * 4,
        out_specs=WHOLE,
        out_shape=jax.ShapeDtypeStruct((2, 4 * ROWS, fields[0].shape[2]), jnp.float32),
        compiler_params=limit(4),
        name="collect",
    )(*fields)


def lane_group():
    return lax.broadcasted_iota(jnp.int32, (100, 128), 1) // 32


def product_kernel(sources, index_ref, *refs):
    blocks, (tx, field, before, o_ref, w_scr, wh_scr, wl_scr) = refs[:-7], refs[-7:]
    tx_index = index_ref[0]
    group = lane_group()
    for g in range(4):
        w_scr[:, ROWS * g + 100 : ROWS * (g + 1), :] = jnp.zeros((2, ROWS - 100, w_scr.shape[2]), jnp.float32)
    for part in range(2):
        for s in range(len(sources)):
            rolled = []
            for k, (ref, place) in enumerate(sources[s]):
                rows = pl.ds(100 * part, 100)
                block = blocks[ref][rows, :] if place is None else blocks[ref][place, rows, :]
                rolled.append(pltpu.roll(block, 32 * k, 1) if k else block)
            for g in range(4):
                mixed = rolled[(0 - g) % 4]
                for lane in range(1, 4):
                    mixed = jnp.where(group == lane, rolled[(lane - g) % 4], mixed)
                if g:
                    mixed = pltpu.roll(mixed, 128 - 32 * g, 1)
                row = pl.multiple_of(jnp.bitwise_xor(tx_index, g) * ROWS, 8)
                w_scr[part, pl.ds(row, 100), 128 * s : 128 * (s + 1)] = mixed
    depth = 128 * len(sources)
    real, imag = w_scr[0], w_scr[1]
    for n, value in enumerate((real + imag, real, imag)):
        high, low = split(value)
        wh_scr[n, :, 0:depth] = high
        wh_scr[n, :, depth:] = high
        wl_scr[n] = low
    for tile in range(field.shape[3] // 256):
        cols = slice(256 * tile, 256 * (tile + 1))
        products = []
        for n in range(3):
            both = field[n, :, :, cols].reshape(2 * depth, 256)
            high = field[n, 1, :, cols]
            products.append(
                jnp.dot(wh_scr[n], both, preferred_element_type=jnp.float32)
                + jnp.dot(wl_scr[n], high, preferred_element_type=jnp.float32)
            )
        a, b = tx[0, :, cols], tx[1, :, cols]
        term = (a - b) * products[0] - b * products[1] - a * products[2]
        o_ref[:, cols] = before[:, cols] + jnp.sum(term, axis=0, keepdims=True)


def product(sources, index, blocks, tx, fields, before):
    edges, depth = fields.shape[3], fields.shape[2]
    return pl.pallas_call(
        functools.partial(product_kernel, sources),
        in_specs=[SCALARS] + [WHOLE] * (len(blocks) + 3),
        out_specs=WHOLE,
        scratch_shapes=[
            pltpu.VMEM((2, 4 * ROWS, depth), jnp.float32),
            pltpu.VMEM((3, 4 * ROWS, 2 * depth), jnp.bfloat16),
            pltpu.VMEM((3, 4 * ROWS, depth), jnp.bfloat16),
        ],
        out_shape=jax.ShapeDtypeStruct((1, edges), jnp.float32),
        compiler_params=limit(12),
        cost_estimate=pl.CostEstimate(flops=3_000_000_000, bytes_accessed=6_000_000, transcendentals=0),
        name="product",
    )(index, *blocks, tx, fields, before)


def onehot_kernel(index_ref, cells_ref, component_ref, hot_ref, row_ref):
    x_lo, core, base, send_x_lo = index_ref[1], index_ref[2], index_ref[3], index_ref[4]
    cells = cells_ref[...] - base
    edges = cells.shape[1]
    lanes = lax.broadcasted_iota(jnp.int32, (128, edges), 0)
    for j in range(4):
        hit = lanes == jnp.bitwise_and(cells[j : j + 1, :], 127)
        hot_ref[j] = jnp.where(hit, 1.0, 0.0).astype(jnp.bfloat16)
    block = cells >> 7
    row = component_ref[...] * 3
    other = 8 * core + 2 * send_x_lo
    row_ref[...] = jnp.where(
        block == 4 + 2 * x_lo + core,
        row,
        jnp.where(block == other + core, row + 1, jnp.where(block == other + 1 - core, row + 2, -1)),
    )


def onehots(index, incidence, component):
    edges = incidence.shape[0]
    return pl.pallas_call(
        onehot_kernel,
        in_specs=[SCALARS, WHOLE, WHOLE],
        out_specs=(WHOLE, WHOLE),
        compiler_params=limit(2),
        out_shape=(
            jax.ShapeDtypeStruct((4, 128, edges), jnp.bfloat16),
            jax.ShapeDtypeStruct((4, edges), jnp.int32),
        ),
        name="onehots",
    )(index, incidence.T, component[None, :])


def scatter_kernel(e0, e1, e2, e3, hot_ref, row_ref, own_ref, send_ref):
    total = 0.25 * ((e0[...] + e1[...]) + (e2[...] + e3[...]))
    edges = total.shape[1]
    rows = lax.broadcasted_iota(jnp.int32, (16, edges), 0)
    first = total.astype(jnp.bfloat16).astype(jnp.float32)
    rest = total - first
    second = rest.astype(jnp.bfloat16).astype(jnp.float32)
    third = rest - second
    summed = jnp.zeros((48, 128), jnp.float32)
    for j in range(4):
        hit = rows == row_ref[j : j + 1, :]
        left = jnp.concatenate([jnp.where(hit, v, 0.0) for v in (first, second, third)], axis=0)
        summed += lax.dot_general(
            left.astype(jnp.bfloat16), hot_ref[j], (((1,), (1,)), ((), ())), preferred_element_type=jnp.float32
        )
    cells = (summed[0:16] + summed[16:32]) + summed[32:48]
    for k in range(3):
        own_ref[k : k + 1, :] = cells[3 * k : 3 * k + 1, :]
        send_ref[0, k : k + 1, :] = cells[3 * k + 1 : 3 * k + 2, :]
        send_ref[1, k : k + 1, :] = cells[3 * k + 2 : 3 * k + 3, :]


def scatter(terms, hot, row):
    return pl.pallas_call(
        scatter_kernel,
        in_specs=[WHOLE] * 6,
        out_specs=(WHOLE, WHOLE),
        compiler_params=limit(4),
        out_shape=(jax.ShapeDtypeStruct((3, 128), jnp.float32), jax.ShapeDtypeStruct((2, 3, 128), jnp.float32)),
        name="scatter_cells",
    )(*terms, hot, row)


def total_kernel(own_ref, received_ref, passed_ref, o_ref):
    o_ref[...] = own_ref[...] + received_ref[0] + passed_ref[...]


def total(own, received, passed):
    return pl.pallas_call(
        total_kernel,
        in_specs=[WHOLE] * 3,
        out_specs=WHOLE,
        compiler_params=limit(2),
        out_shape=jax.ShapeDtypeStruct(own.shape, jnp.float32),
        name="total",
    )(own, received, passed)


def neighbour_parts(block):
    route = []
    for m in range(64):
        for j in range(4):
            source = m + 1 if j % 2 == 0 else m - 1
            flip = 2 if {m, source} == {31, 32} else 0
            if 0 <= source < 64:
                route.append((source * 4 + (j ^ flip), m * 4 + j))
    return lax.ppermute(block, AXES, route)


def flip_x(x_hi, z, y, x_lo, core):
    return x_hi, z, y, 1 - x_lo, core


def flip_core(x_hi, z, y, x_lo, core):
    return x_hi, z, y, x_lo, 1 - core


def flip_both(x_hi, z, y, x_lo, core):
    return x_hi, z, y, 1 - x_lo, 1 - core


def z_source(k):
    def source(x_hi, z, y, x_lo, core):
        if z // 4 == core:
            return x_lo, 4 * core + ((z % 4) ^ NEAR_TURNS[k]), y, x_hi, 1 - core
        return x_lo, 4 * core + ((z % 4) ^ FAR_TURNS[k]), y, x_hi, core

    return source


def y_partner(pairs, y):
    return (y ^ 1) if pairs == 0 else (y + 2 * (y % 2) - 1) % SIZE_Y


def y_source(pairs):
    return lambda x_hi, z, y, x_lo, core: (x_hi, z, y_partner(pairs, y), x_lo, core)


def shards(tx_field, rx_field, misfit_weight, incidence, component):
    mesh_index = lax.axis_index("mesh")
    tx_index = lax.axis_index("tx")
    z, y = (mesh_index // 4) % 8, mesh_index % 4
    packed = pack_weight(misfit_weight)
    tx_own = tx_field.transpose(1, 0, 2)
    tx_x = fetch(tx_own, flip_x)
    from_z = [fetch(packed, z_source(k)) for k in range(4)]
    y_places = [y, y_partner(0, y), y_partner(1, y), (y + 2) % SIZE_Y]
    same_half = z // 4 == tx_index % 2
    z_places = [(z % 4) ^ jnp.where(same_half, NEAR_TURNS[k], FAR_TURNS[k]) for k in range(4)]
    places = jnp.stack(z_places + y_places).astype(jnp.int32)
    x_lo, core = tx_index // 2, tx_index % 2
    flipped = mesh_index == jnp.where(core == 0, 32, 31)
    send_x_lo = jnp.where(flipped, 1 - x_lo, x_lo)
    index = jnp.stack([tx_index, x_lo, core, (mesh_index - 1) * CELL_TILE, send_x_lo]).astype(jnp.int32)
    hot, row = onehots(index, incidence, component)

    stacked = [jnp.stack(from_z[2 * g : 2 * g + 2]) for g in range(2)]
    tx_c = fetch(tx_own, flip_core)
    tx_x = gate(stacked, tx_x)
    tx_xc = fetch(tx_x, flip_core)
    near = [fetch(stacked[g], y_source(0)) for g in range(2)]
    far = [fetch(stacked[g], y_source(1)) for g in range(2)]
    last = [fetch(near[0], y_source(1)), fetch(far[1], y_source(0))]
    fields = prepare_fields(places, rx_field)
    tx = collect(tx_own, tx_c, tx_x, tx_xc)
    edge = jnp.zeros((1, tx_field.shape[2]), jnp.float32)
    pairs = lambda first: [(first, 0), (first, 1), (first + 1, 0), (first + 1, 1)]
    early = [[(k, None) for k in range(4)], pairs(4)]
    edge = product(early, index, from_z + [near[0], far[1]], tx, fields[0], edge)
    edge = product([pairs(0), pairs(2)], index, [far[0], near[1]] + last, tx, fields[1], edge)
    terms = [edge, fetch(edge, flip_x), fetch(edge, flip_both), fetch(edge, flip_core)]
    own, send = scatter(terms, hot, row)
    received = neighbour_parts(send)
    return total(own, received, fetch(received[1], flip_core))


def solution(mesh):
    return jax.shard_map(
        shards,
        mesh=mesh,
        in_specs=(
            P(None, "tx", "mesh"),
            P(None, "tx", "mesh"),
            P(None, None, "mesh"),
            P("mesh", None),
            P("mesh"),
        ),
        out_specs=P(None, ("mesh", "tx")),
        check_vma=False,
    )
```
